768 devices in a mesh: row: 96 (over z, y), col: 8 (over x, core).
Axes of the slice: x: 4, y: 8, z: 12, core: 2. Of those that a mesh axis runs over, the one named last changes fastest.
Arguments:
- pooled_grad: bfloat16 [3072, 8, 512], P(('row', 'col')), may hold values from -6 to 6
- cold_table: float32 [512, 196608], P('col', 'row'), may hold values from -4 to 4
- cold_accum: float32 [196608], P('row'), may hold values from 0.05 to 0.5
- hot_table: float32 [512, 192], P('col'), may hold values from -4 to 4
- hot_accum: float32 [192], replicated, may hold values from 0.05 to 0.5
- cold_owner: int32 [36864, 1], P('row'), may hold values from 0 to 95; in each aligned block of 384 rows (0 to 383, 384 to 767, ...) at most 8 rows name the same one
- cold_row: int32 [36864], P('row'), may hold values from 0 to 2047
- cold_bag: int32 [36864], P('row'), may hold values from 0 to 255
- hot_id: int32 [49152], P('row'), may hold values from 0 to 191
- hot_bag: int32 [49152], P('row'), may hold values from 0 to 255
Outputs:
- new_cold: float32 [512, 196608], P('col', 'row')
- new_cold_accum: float32 [196608], P('row')
- new_hot: float32 [512, 192], P('col')
- new_hot_accum: float32 [192], replicated
The draws below stay inside these ranges and needn't reach their ends.
Inputs may be any that keep to these rules, and one draw needn't show every extreme that they name: `cold_owner`: within the rows of one device, at most 8 lookups name one owner, and in every draw some owner is named by exactly 8 of them.
All inputs are finite; a program needn't handle non-finite values.
Results may differ from the reference program's by a relative error of at most 0.0003.
Values may be sent and summed in bfloat16 or wider, within the bound.
A program may use at most 32 MiB of HBM per device.

```python
import math
import jax
import jax.numpy as jnp
import numpy as np
from jax import lax

E = 512
F_W = 8
SAMP_DEV = 32
LK_DEV = 384
LH_DEV = 512
V_DEV = 2048
HOT_PER = 2
BAGS_DEV = 256
CAP = 8
B = 3072
V = 196608
H = 192
LK = 36864
LH = 49152
N_ROW = 96


def touch_ends(array, rng, least, top_value):
    extent = array.shape
    place = [jax.random.randint(jax.random.fold_in(rng, axis), (), 0, extent[axis]) for axis in range(len(extent))]
    array = array.at[tuple(place)].set(least)
    longest = extent.index(max(extent))
    place[longest] = (place[longest] + 1) % extent[longest]
    return array.at[tuple(place)].set(top_value)


def block_scale(own_key, extent, pieces, least, top_value):
    level, own = 1.0, jax.random.fold_in(own_key, 6)
    for dim, shards_of in pieces:
        draws = jnp.exp(jax.random.uniform(jax.random.fold_in(own, dim), (shards_of,), jnp.float32, least / len(pieces), top_value / len(pieces)))
        level = level * jnp.repeat(draws, extent[dim] // shards_of).reshape([-1 if axis == dim else 1 for axis in range(len(extent))])
    return level


def shared_out(own_key, own, number, rows, number_of, top, limit, slope):
    ranking = jax.random.permutation(own_key, number_of)
    heavy_load, usual = portions_of(number_of, rows * top, limit, slope, True), portions_of(number_of, rows * top, limit, slope, False)
    places = jnp.arange(number_of)

    def named(lengths, rotation):
        used = int((lengths > 0).sum())
        fixed = max(1, used // 4)
        passed = fixed + (places - fixed + rotation * (used - fixed)) % max(1, number_of - fixed)
        return jnp.zeros((number_of,), jnp.int32).at[ranking[jnp.where(places < fixed, places, passed)]].set(jnp.asarray(lengths, jnp.int32))

    lengths = jnp.where(number % 4 == 0, named(heavy_load, number // 4), named(usual, number - number // 4 - 1))
    mixed = jax.random.permutation(jax.random.fold_in(own, 3), number_of)
    source_of, taker = mixed[0:number_of // 2 * 2:2], mixed[1:number_of // 2 * 2:2]
    margin = jnp.minimum(lengths[source_of] - 1, limit - lengths[taker]) // 2
    margin = jnp.where((source_of == ranking[0]) | (taker == ranking[0]) | (lengths[taker] == 0), 0, jnp.maximum(margin, 0))
    passed = jax.random.randint(jax.random.fold_in(own, 4), (number_of // 2,), 0, 1 << 20) % (margin + 1)
    lengths = lengths.at[source_of].add(-passed).at[taker].add(passed)
    members = jnp.searchsorted(jnp.cumsum(lengths), jnp.arange(rows * top), side="right").astype(jnp.int32)
    grid = members.reshape(top, rows).T
    grid = grid[jax.random.permutation(jax.random.fold_in(own, 1), rows)]
    rotation = jax.random.randint(jax.random.fold_in(own, 2), (rows, 1), 0, top)
    return jnp.take_along_axis(grid, (jnp.arange(top)[None, :] + rotation) % top, axis=1)


def portions_of(amount, total, limit, skew, full):
    portions = [(1 << 20) // math.isqrt(grade ** skew) + 1 for grade in range(1, amount + 1)]
    largest = limit if full else min(limit, max(-(-total // amount), total * portions[0] // sum(portions)))
    least = 1 if total - largest >= amount - 1 else 0
    given, spare = [largest] + [least] * (amount - 1), total - largest - least * (amount - 1)
    while spare > 0:
        free = [i for i in range(1, amount) if given[i] < largest] or [i for i in range(1, amount) if given[i] < limit]
        whole, left = sum([portions[i] for i in free]), spare
        for i in free:
            more = min(limit - given[i], max(1, left * portions[i] // whole), spare)
            given[i] = given[i] + more
            spare = spare - more
    return np.array(given)


def scatter_about(own_key, shape, spread, limit, cuts=(), dtype=jnp.bfloat16):
    gain = block_scale(own_key, shape, cuts, -0.22, 0.18) if cuts else 1.0
    entries = jax.random.normal(own_key, shape, jnp.float32) * spread * gain
    return jnp.minimum(jnp.maximum(entries, -limit), limit).astype(dtype)


def setup_inputs(seed: int = 0) -> dict:
    splits = jax.random.split(jax.random.key(seed), 11)
    pooled_grad = scatter_about(splits[0], (B, F_W, E), 1.0, 6.0, ((0, 768),))
    cold_table = scatter_about(splits[1], (E, V), 0.5, 4.0, ((0, 8), (1, 96)), jnp.float32)
    cold_accum = jnp.clip(jnp.exp(math.log(0.5) - 2.3025851 * jax.random.uniform(splits[2], (V,), jnp.float32) ** block_scale(splits[2], (V,), ((0, 96),), -0.2, 0.2)), 0.05, 0.5)
    hot_table = scatter_about(splits[3], (E, H), 0.5, 4.0, ((0, 8),), jnp.float32)
    hot_accum = jnp.clip(jnp.exp(jax.random.uniform(splits[4], (H,), jnp.float32, math.log(0.05), math.log(0.5))), 0.05, 0.5)
    cold_owner_keys = jax.random.split(jax.random.fold_in(splits[5], 1), LK // LK_DEV)
    cold_owner_turns = jax.random.permutation(jax.random.fold_in(splits[5], 3), LK // LK_DEV)
    cold_owner = jax.vmap(lambda own, number: shared_out(jax.random.fold_in(splits[5], 2), own, number, LK_DEV, N_ROW, 1, CAP, 2))(cold_owner_keys, cold_owner_turns).reshape((LK, 1))
    cold_row = touch_ends(jax.random.randint(splits[6], (LK,), 0, V_DEV), jax.random.fold_in(splits[6], 1), 0, V_DEV - 1).astype(jnp.int32)
    cold_bag = touch_ends(jax.random.randint(splits[7], (LK,), 0, BAGS_DEV), jax.random.fold_in(splits[7], 1), 0, BAGS_DEV - 1).astype(jnp.int32)
    hot_id = touch_ends(jax.random.randint(splits[8], (LH,), 0, H), jax.random.fold_in(splits[8], 1), 0, H - 1).astype(jnp.int32)
    hot_bag = touch_ends(jax.random.randint(splits[9], (LH,), 0, BAGS_DEV), jax.random.fold_in(splits[9], 1), 0, BAGS_DEV - 1).astype(jnp.int32)
    return {"pooled_grad": pooled_grad, "cold_table": cold_table, "cold_accum": cold_accum, "hot_table": hot_table, "hot_accum": hot_accum, "cold_owner": cold_owner, "cold_row": cold_row, "cold_bag": cold_bag, "hot_id": hot_id, "hot_bag": hot_bag}


LR = 0.3
EPS = 1e-08

def adagrad(table, accum, grad):
    new_accum = accum + lax.optimization_barrier(jnp.sum(grad * grad, axis=1)) / E
    new_table = table - LR * (grad / (jnp.sqrt(new_accum) + EPS)[:, None]).T
    return (new_table, new_accum)

def reference(pooled_grad, cold_table, cold_accum, hot_table, hot_accum, cold_owner, cold_row, cold_bag, hot_id, hot_bag):
    bags = pooled_grad.astype(jnp.float32).reshape(-1, E)
    bags_dev = SAMP_DEV * F_W
    cold_dev = (jnp.arange(N_ROW * LK_DEV) // LK_DEV).astype(jnp.int32)
    cold_global = cold_dev * bags_dev + cold_bag.astype(jnp.int32)
    cold_target = cold_owner[:, 0].astype(jnp.int32) * V_DEV + cold_row.astype(jnp.int32)
    cold_grad = jax.ops.segment_sum(bags[cold_global], cold_target, num_segments=N_ROW * V_DEV)
    hot_dev = (jnp.arange(N_ROW * LH_DEV) // LH_DEV).astype(jnp.int32)
    hot_global = hot_dev * bags_dev + hot_bag.astype(jnp.int32)
    hot_grad = jax.ops.segment_sum(bags[hot_global], hot_id.astype(jnp.int32), num_segments=HOT_PER * N_ROW)
    new_cold, new_cold_accum = adagrad(cold_table, cold_accum, cold_grad)
    new_hot, new_hot_accum = adagrad(hot_table, hot_accum, hot_grad)
    return (new_cold, new_cold_accum, new_hot, new_hot_accum)
```

```python
import jax
import jax.numpy as jnp
from jax import lax
from jax.sharding import PartitionSpec as P

E = 512


LR = 0.3
EPS = 1e-08


def adagrad(table, accum, grad, squares):
    new_accum = accum + squares / E
    new_table = table - LR * grad / (jnp.sqrt(new_accum) + EPS)[None, :]
    return (new_table, new_accum)


def expand(bag_index, bags):
    picker = (bag_index[:, None] == jnp.arange(bags.shape[0], dtype=jnp.int32)[None, :]).astype(
        jnp.bfloat16
    )
    return jnp.dot(picker, bags, preferred_element_type=jnp.float32).astype(jnp.bfloat16)


def contract_lookups(values, placer):
    return lax.dot_general(
        values, placer, (((0,), (0,)), ((), ())), preferred_element_type=jnp.float32
    )


def on_device(
    pooled_grad,
    cold_table,
    cold_accum,
    hot_table,
    hot_accum,
    cold_owner,
    cold_row,
    cold_bag,
    hot_id,
    hot_bag,
):
    num_rows = lax.axis_size("row")
    columns = lax.all_to_all(pooled_grad, "col", split_axis=2, concat_axis=0, tiled=True)
    bags = columns.reshape(-1, columns.shape[2])
    expanded = expand(cold_bag, bags)
    owner = cold_owner[:, 0]
    lookups = owner.shape[0]
    capacity = 2 * lookups // num_rows
    target = (owner[:, None] == jnp.arange(num_rows, dtype=jnp.int32)[None, :]).astype(jnp.int32)
    rank = jnp.sum((jnp.cumsum(target, axis=0) - 1) * target, axis=1)
    slot = owner * capacity + rank
    placed = slot[None, :] == jnp.arange(num_rows * capacity, dtype=jnp.int32)[:, None]
    outgoing = jnp.dot(
        placed.astype(jnp.bfloat16), expanded, preferred_element_type=jnp.float32
    ).astype(jnp.bfloat16)
    out_rows = jnp.sum(jnp.where(placed, cold_row[None, :] + 1, 0), axis=1) - 1
    arrived, arrived_rows = (
        lax.all_to_all(outgoing, "row", split_axis=0, concat_axis=0, tiled=True),
        lax.all_to_all(out_rows, "row", split_axis=0, concat_axis=0, tiled=True),
    )
    local_rows = cold_table.shape[1]
    landing = (arrived_rows[:, None] == jnp.arange(local_rows, dtype=jnp.int32)[None, :]).astype(
        jnp.bfloat16
    )
    cold_grad = contract_lookups(arrived, landing)
    cold_squares = jnp.sum(cold_grad * cold_grad, axis=0)
    hot_expanded = expand(hot_bag, bags)
    hot_count = hot_table.shape[1]
    hot_place = (hot_id[:, None] == jnp.arange(hot_count, dtype=jnp.int32)[None, :]).astype(
        jnp.bfloat16
    )
    hot_partial = contract_lookups(hot_expanded, hot_place)
    pieces = lax.all_to_all(hot_partial.T, "row", split_axis=0, concat_axis=0, tiled=True)
    own_sum = jnp.sum(pieces.reshape(num_rows, hot_count // num_rows, -1), axis=0)
    spread = jnp.broadcast_to(own_sum[None], (num_rows,) + own_sum.shape)
    hot_grad = lax.all_to_all(spread, "row", split_axis=0, concat_axis=0, tiled=True)
    hot_grad = hot_grad.reshape(hot_count, -1).T
    cold_total, hot_total = lax.psum((cold_squares, jnp.sum(hot_grad * hot_grad, axis=0)), "col")
    new_hot, new_hot_accum = adagrad(hot_table, hot_accum, hot_grad, hot_total)
    new_cold, new_cold_accum = adagrad(cold_table, cold_accum, cold_grad, cold_total)
    return (new_cold, new_cold_accum, new_hot, new_hot_accum)


def solution(mesh):
    in_specs = (
        P(("row", "col"), None, None),
        P("col", "row"),
        P("row"),
        P("col", None),
        P(),
        P("row", None),
        P("row"),
        P("row"),
        P("row"),
        P("row"),
    )
    out_specs = (P("col", "row"), P("row"), P("col", None), P())
    return jax.shard_map(
        on_device, mesh=mesh, in_specs=in_specs, out_specs=out_specs, check_vma=False
    )
```

```python
import jax
import jax.numpy as jnp
from jax import lax
from jax.experimental import pallas as pl
from jax.experimental.pallas import tpu as pltpu
from jax.sharding import PartitionSpec as P

E = 512
LR = 0.3
EPS = 1e-08
MESH = pl.DeviceIdType.MESH

NC = 8
NY = 8
NZ = 12
LK = 384
LH = 512
CAP = 8
F32 = jnp.float32
BF16 = jnp.bfloat16


def iota(shape, dim):
    return lax.broadcasted_iota(jnp.int32, shape, dim)


def one_hot(mask):
    return jnp.where(mask, 1.0, 0.0).astype(BF16)


def dot(a, b):
    return jnp.dot(a, b, preferred_element_type=F32)


def dot_t(a, b):
    return lax.dot_general(a, b, (((1,), (1,)), ((), ())), preferred_element_type=F32)


def exchange_kernel(
    pool_ref,
    owner_ref,
    row_ref,
    bag_ref,
    hot_id_ref,
    hot_bag_ref,
    grad_ref,
    cold_total_ref,
    hot_grad_ref,
    hot_total_ref,
    bags_send,
    bags_recv,
    rows_y_send,
    rows_y_recv,
    rows_z_send,
    rows_z_recv,
    cold_y_send,
    cold_y_recv,
    cold_z_send,
    cold_z_recv,
    hot_z_send,
    hot_z_recv,
    hot_y_recv,
    hot_all_recv,
    square_recv,
    send_sems,
    recv_sems,
):
    row = lax.axis_index("row")
    col = lax.axis_index("col")
    z = lax.div(row, NY)
    y = lax.rem(row, NY)

    def along_col(k):
        other = lax.rem(col + k, NC)
        return other, {"row": row, "col": other}

    def along_y(k):
        other = lax.rem(y + k, NY)
        return other, {"row": z * NY + other, "col": col}

    def along_z(k):
        other = lax.rem(z + k, NZ)
        return other, {"row": other * NY + y, "col": col}

    def start(stage, count, along, me, send, recv):
        for k in range(1, count):
            other, device = along(k)
            pltpu.make_async_remote_copy(
                src_ref=send.at[me if send is recv else other],
                dst_ref=recv.at[me],
                send_sem=send_sems.at[stage],
                recv_sem=recv_sems.at[stage],
                device_id=device,
                device_id_type=MESH,
            ).start()

    def wait(sem, count, ref):
        part = ref.at[pl.ds(0, count - 1)]
        pltpu.make_async_copy(part, part, sem).wait()

    barrier = pltpu.get_barrier_semaphore()
    for count, along in ((NC, along_col), (NY, along_y), (NZ, along_z)):
        for k in range(1, count):
            pl.semaphore_signal(barrier, inc=1, device_id=along(k)[1], device_id_type=MESH)

    low_lanes = iota((16, 128), 1) < 64
    for pair in range(NC // 2):
        first = pool_ref[0:16, pair * 128 : pair * 128 + 128].astype(F32)
        second = pool_ref[16:32, pair * 128 : pair * 128 + 128].astype(F32)
        bags_send[2 * pair] = jnp.where(low_lanes, first, pltpu.roll(second, 64, 1)).astype(BF16)
        bags_send[2 * pair + 1] = jnp.where(low_lanes, pltpu.roll(first, 64, 1), second).astype(BF16)
    bags_recv[col] = bags_send[col]
    pl.semaphore_wait(barrier, NC + NY + NZ - 3)
    start(0, NC, along_col, col, bags_send, bags_recv)

    owner = owner_ref[...].reshape(1, LK)
    target = iota((NY * NZ, LK), 0) == owner
    earlier = one_hot(iota((LK, LK), 0) < iota((LK, LK), 1))
    before = dot(one_hot(target), earlier)
    rank = jnp.sum(jnp.where(target, before, 0.0), axis=0, keepdims=True).astype(jnp.int32)
    owner_z, owner_y = owner >> 3, owner & 7
    half, quarter = rank >> 2, rank & 3
    table_row = row_ref[...].reshape(1, LK)
    line = owner_y * (2 * NZ) + owner_z * 2 + half
    lane = lax.rem(z, 4) * 32 + y * 4 + quarter
    in_lane = iota((128, LK), 0) == lane
    high = jnp.where(in_lane, (table_row >> 8) + 1, 0).astype(F32).astype(BF16)
    low = jnp.where(in_lane, table_row & 255, 0).astype(F32).astype(BF16)
    in_line = one_hot(iota((NY * NZ * 2, LK), 0) == line)
    codes = dot_t(in_line, high) * 256.0 + dot_t(in_line, low)
    rows_y_send[...] = codes.reshape(NY, 2 * NZ, 128)
    rows_y_recv[y] = rows_y_send[y]
    start(1, NY, along_y, y, rows_y_send, rows_y_recv)

    def place_of_bag(bag):
        return ((bag >> 4) & 1) * 128 + (bag >> 5) * 16 + (bag & 15)

    position = owner_y * (NZ * 4) + owner_z * 4 + quarter + half * LK
    placed = one_hot(iota((2 * LK, LK), 0) == position)
    cold_place = place_of_bag(bag_ref[...].reshape(1, LK)) + 1
    cold_place = jnp.broadcast_to(cold_place, (8, LK)).astype(F32).astype(BF16)
    slot_place = dot_t(placed, cold_place)[:, 0:1].astype(jnp.int32)
    bag_number = iota((LK, 256), 1) + 1
    pick = jnp.concatenate(
        [one_hot(slot_place[:LK] == bag_number), one_hot(slot_place[LK:] == bag_number)], axis=1
    )

    hot_id = hot_id_ref[...].reshape(1, LH)
    hot_line = (hot_id >> 4) * 8 + (hot_id & 7) + ((hot_id >> 3) & 1) * (NZ * 8)
    hot_rows = one_hot(iota((NZ * 16, LH), 0) == hot_line)
    hot_place = place_of_bag(hot_bag_ref[...].reshape(1, LH))
    counts = dot_t(hot_rows, one_hot(iota((256, LH), 0) == hot_place))
    counts = jnp.concatenate([counts[: NZ * 8], counts[NZ * 8 :]], axis=1)
    count_high = counts.astype(BF16)
    count_low = (counts - count_high.astype(F32)).astype(BF16)

    wait(recv_sems.at[0], NC, bags_recv)
    bags = bags_recv[...].reshape(128, 128).astype(F32)
    rolled = pltpu.roll(bags, 64, 1)
    left = iota((128, 128), 1) < 64
    spread = jnp.concatenate(
        [
            jnp.where(left, bags, 0.0),
            jnp.where(left, rolled, 0.0),
            jnp.where(left, 0.0, rolled),
            jnp.where(left, 0.0, bags),
        ],
        axis=0,
    ).astype(BF16)
    cold_y_send[...] = dot(pick, spread).astype(BF16).reshape(NY, NZ * 4, 128)
    cold_y_recv[y] = cold_y_send[y]
    start(2, NY, along_y, y, cold_y_send, cold_y_recv)
    hot_z_send[...] = (dot(count_high, spread) + dot(count_low, spread)).reshape(NZ, 8, 128)
    hot_z_recv[z] = hot_z_send[z]
    start(3, NZ, along_z, z, hot_z_send, hot_z_recv)

    wait(recv_sems.at[1], NY, rows_y_recv)
    merged = jnp.sum(rows_y_recv[...], axis=0)
    for other in range(NZ):
        rows_z_send[other, 0:2] = merged[2 * other : 2 * other + 2]
        rows_z_send[other, 2:8] = jnp.zeros((6, 128), F32)
    rows_z_recv[z] = rows_z_send[z]
    start(4, NZ, along_z, z, rows_z_send, rows_z_recv)

    out_row = iota((LK, LK), 0)
    source = ((out_row >> 2) & 7) * (NZ * 4) + (out_row >> 5) * 4 + (out_row & 3)
    regroup = one_hot(iota((LK, LK), 1) == source)

    wait(recv_sems.at[2], NY, cold_y_recv)
    regrouped = dot(regroup, cold_y_recv[...].reshape(LK, 128)).astype(BF16)
    cold_z_send[...] = regrouped.reshape(NZ, 32, 128)
    cold_z_recv[z] = cold_z_send[z]
    start(5, NZ, along_z, z, cold_z_send, cold_z_recv)

    wait(recv_sems.at[3], NZ, hot_z_recv)
    hot_y_recv[y] = jnp.sum(hot_z_recv[...], axis=0)
    start(6, NY, along_y, y, hot_y_recv, hot_y_recv)

    wait(recv_sems.at[4], NZ, rows_z_recv)
    code = jnp.concatenate(
        [jnp.sum(rows_z_recv[4 * g : 4 * g + 4], axis=0) for g in range(NZ // 4)], axis=1
    ).astype(jnp.int32)
    code_high, code_low = code >> 8, code & 255
    low_number = iota((256, LK), 0)
    land = [one_hot(code_low[side : side + 1] == low_number) for side in range(2)]

    wait(recv_sems.at[6], NY, hot_y_recv)
    hot_all_recv[z] = jnp.sum(hot_y_recv[...], axis=0)
    start(7, NZ, along_z, z, hot_all_recv, hot_all_recv)

    wait(recv_sems.at[5], NZ, cold_z_recv)
    arrived = cold_z_recv[...].reshape(LK, 128).astype(F32).T
    grads = jnp.zeros((512, 256), F32)
    for side in range(2):
        mine = arrived[64 * side : 64 * side + 64]
        masked = jnp.concatenate(
            [jnp.where(code_high[side : side + 1] == h + 1, mine, 0.0) for h in range(8)], axis=0
        ).astype(BF16)
        grads += dot_t(masked, land[side])
    squares = []
    for h in range(8):
        part = grads[64 * h : 64 * h + 64]
        grad_ref[:, 256 * h : 256 * h + 256] = part
        squares.append(jnp.sum(part * part, axis=0, keepdims=True))
    square_recv[col, :, 0:256] = jnp.concatenate(squares, axis=0)

    wait(recv_sems.at[7], NZ, hot_all_recv)
    pieces = []
    for other in range(NZ):
        piece = hot_all_recv[other]
        pieces += [piece, pltpu.roll(piece, 64, 1)]
    hot_grad = jnp.concatenate(pieces + [jnp.zeros((64, 128), F32)], axis=0).T[0:64]
    hot_grad_ref[...] = hot_grad
    hot_squares = jnp.sum(hot_grad * hot_grad, axis=0, keepdims=True)
    square_recv[col, :, 256:384] = jnp.concatenate(
        [hot_squares[:, 0:128], hot_squares[:, 128:256], jnp.zeros((6, 128), F32)], axis=0
    )
    start(8, NC, along_col, col, square_recv, square_recv)
    wait(recv_sems.at[8], NC, square_recv)
    total = square_recv[0]
    for other in range(1, NC):
        total += square_recv[other]
    cold_total_ref[...] = total[:, 0:256]
    hot_total_ref[...] = total[:, 256:384]

    for stage, count, send in (
        (0, NC, bags_send),
        (1, NY, rows_y_send),
        (2, NY, cold_y_send),
        (3, NZ, hot_z_send),
        (4, NZ, rows_z_send),
        (5, NZ, cold_z_send),
        (6, NY, hot_y_recv),
        (7, NZ, hot_all_recv),
        (8, NC, square_recv),
    ):
        wait(send_sems.at[stage], count, send)


def exchange(pool, owner, cold_row, cold_bag, hot_id, hot_bag):
    vmem = pl.BlockSpec(memory_space=pltpu.VMEM)
    return pl.pallas_call(
        exchange_kernel,
        out_shape=(
            jax.ShapeDtypeStruct((64, 2048), F32),
            jax.ShapeDtypeStruct((8, 256), F32),
            jax.ShapeDtypeStruct((64, 256), F32),
            jax.ShapeDtypeStruct((8, 128), F32),
        ),
        in_specs=[vmem] * 6,
        out_specs=(vmem,) * 4,
        scratch_shapes=[
            pltpu.VMEM((NC, 16, 128), BF16),
            pltpu.VMEM((NC, 16, 128), BF16),
            pltpu.VMEM((NY, 2 * NZ, 128), F32),
            pltpu.VMEM((NY, 2 * NZ, 128), F32),
            pltpu.VMEM((NZ, 8, 128), F32),
            pltpu.VMEM((NZ, 8, 128), F32),
            pltpu.VMEM((NY, NZ * 4, 128), BF16),
            pltpu.VMEM((NY, NZ * 4, 128), BF16),
            pltpu.VMEM((NZ, 32, 128), BF16),
            pltpu.VMEM((NZ, 32, 128), BF16),
            pltpu.VMEM((NZ, 8, 128), F32),
            pltpu.VMEM((NZ, 8, 128), F32),
            pltpu.VMEM((NY, 8, 128), F32),
            pltpu.VMEM((NZ, 8, 128), F32),
            pltpu.VMEM((NC, 8, 384), F32),
            pltpu.SemaphoreType.DMA((9,)),
            pltpu.SemaphoreType.DMA((9,)),
        ],
        compiler_params=pltpu.CompilerParams(
            collective_id=0, has_side_effects=True, vmem_limit_bytes=32 * 1024 * 1024
        ),
        name="exchange",
    )(pool, owner, cold_row, cold_bag, hot_id, hot_bag)


def update_kernel(
    table_ref,
    accum_ref,
    grad_ref,
    total_ref,
    hot_table_ref,
    hot_accum_ref,
    hot_grad_ref,
    hot_total_ref,
    new_ref,
    new_accum_ref,
    new_hot_ref,
    new_hot_accum_ref,
):
    for h in range(8):
        at = slice(256 * h, 256 * h + 256)
        accum = accum_ref[at].reshape(1, 256) + total_ref[h : h + 1, :] / E
        new_accum_ref[at] = accum.reshape(256)
        scale = LR / (jnp.sqrt(accum) + EPS)
        new_ref[:, at] = table_ref[:, at] - grad_ref[:, at] * scale
    hot_total = jnp.concatenate([hot_total_ref[0:1, :], hot_total_ref[1:2, 0:64]], axis=1)
    accum = hot_accum_ref[...].reshape(1, 192) + hot_total / E
    new_hot_accum_ref[...] = accum.reshape(192)
    new_hot_ref[...] = hot_table_ref[...] - hot_grad_ref[:, 0:192] * (
        LR / (jnp.sqrt(accum) + EPS)
    )


def update(table, accum, grad, total, hot_table, hot_accum, hot_grad, hot_total):
    vmem = pl.BlockSpec(memory_space=pltpu.VMEM)
    return pl.pallas_call(
        update_kernel,
        out_shape=(
            jax.ShapeDtypeStruct(table.shape, F32),
            jax.ShapeDtypeStruct(accum.shape, F32),
            jax.ShapeDtypeStruct(hot_table.shape, F32),
            jax.ShapeDtypeStruct(hot_accum.shape, F32),
        ),
        in_specs=[vmem] * 8,
        out_specs=(vmem,) * 4,
        compiler_params=pltpu.CompilerParams(vmem_limit_bytes=16 * 1024 * 1024),
        name="update",
    )(table, accum, grad, total, hot_table, hot_accum, hot_grad, hot_total)


def on_device(
    pooled_grad,
    cold_table,
    cold_accum,
    hot_table,
    hot_accum,
    cold_owner,
    cold_row,
    cold_bag,
    hot_id,
    hot_bag,
):
    grad, total, hot_grad, hot_total = exchange(
        pooled_grad.reshape(32, E), cold_owner.T, cold_row, cold_bag, hot_id, hot_bag
    )
    return tuple(
        update(cold_table, cold_accum, grad, total, hot_table, hot_accum, hot_grad, hot_total)
    )


def solution(mesh):
    in_specs = (
        P(("row", "col"), None, None),
        P("col", "row"),
        P("row"),
        P("col", None),
        P(),
        P("row", None),
        P("row"),
        P("row"),
        P("row"),
        P("row"),
    )
    out_specs = (P("col", "row"), P("row"), P("col", None), P())
    return jax.shard_map(
        on_device, mesh=mesh, in_specs=in_specs, out_specs=out_specs, check_vma=False
    )
```

```python
import jax
import jax.numpy as jnp
from jax import lax
from jax.experimental import pallas as pl
from jax.experimental.pallas import tpu as pltpu
from jax.sharding import PartitionSpec as P

E = 512
LR = 0.3
EPS = 1e-08
MESH = pl.DeviceIdType.MESH

NC = 8
NY = 8
NZ = 12
LK = 384
LH = 512
CAP = 8
F32 = jnp.float32
BF16 = jnp.bfloat16


def iota(shape, dim):
    return lax.broadcasted_iota(jnp.int32, shape, dim)


def one_hot(mask):
    return jnp.where(mask, 1.0, 0.0).astype(BF16)


def dot(a, b):
    return jnp.dot(a, b, preferred_element_type=F32)


def dot_t(a, b):
    return lax.dot_general(a, b, (((1,), (1,)), ((), ())), preferred_element_type=F32)


def exchange_kernel(
    pool_hbm,
    owner_hbm,
    row_hbm,
    bag_hbm,
    hot_id_hbm,
    hot_bag_hbm,
    table_hbm,
    accum_hbm,
    hot_table_hbm,
    hot_accum_hbm,
    new_hbm,
    new_accum_hbm,
    new_hot_hbm,
    new_hot_accum_hbm,
    pool_ref,
    owner_ref,
    row_ref,
    bag_ref,
    hot_id_ref,
    hot_bag_ref,
    table_ref,
    accum_ref,
    hot_table_ref,
    hot_accum_ref,
    new_ref,
    new_accum_ref,
    new_hot_ref,
    new_hot_accum_ref,
    grad_ref,
    bags_send,
    bags_recv,
    rows_y_send,
    rows_y_recv,
    rows_z_send,
    rows_z_recv,
    cold_y_send,
    cold_y_recv,
    cold_z_send,
    cold_z_recv,
    hot_z_send,
    hot_z_recv,
    hot_y_recv,
    hot_all_recv,
    square_recv,
    fetch_sems,
    store_sems,
    send_sems,
    recv_sems,
):
    row = lax.axis_index("row")
    col = lax.axis_index("col")
    z = lax.div(row, NY)
    y = lax.rem(row, NY)

    def along_col(k):
        other = lax.rem(col + k, NC)
        return other, {"row": row, "col": other}

    def along_y(k):
        other = lax.rem(y + k, NY)
        return other, {"row": z * NY + other, "col": col}

    def along_z(k):
        other = lax.rem(z + k, NZ)
        return other, {"row": other * NY + y, "col": col}

    def start(stage, count, along, me, send, recv):
        for k in range(1, count):
            other, device = along(k)
            pltpu.make_async_remote_copy(
                src_ref=send.at[me if send is recv else other],
                dst_ref=recv.at[me],
                send_sem=send_sems.at[stage],
                recv_sem=recv_sems.at[stage],
                device_id=device,
                device_id_type=MESH,
            ).start()

    def wait(sem, count, ref):
        part = ref.at[pl.ds(0, count - 1)]
        pltpu.make_async_copy(part, part, sem).wait()

    barrier = pltpu.get_barrier_semaphore()
    for count, along in ((NC, along_col), (NY, along_y), (NZ, along_z)):
        for k in range(1, count):
            pl.semaphore_signal(barrier, inc=1, device_id=along(k)[1], device_id_type=MESH)

    fetches = [
        pltpu.make_async_copy(source, target, fetch_sems.at[i])
        for i, (source, target) in enumerate(
            (
                (pool_hbm, pool_ref),
                (owner_hbm, owner_ref),
                (row_hbm, row_ref),
                (bag_hbm, bag_ref),
                (hot_id_hbm, hot_id_ref),
                (hot_bag_hbm, hot_bag_ref),
                (table_hbm, table_ref),
                (accum_hbm, accum_ref),
                (hot_table_hbm, hot_table_ref),
                (hot_accum_hbm, hot_accum_ref),
            )
        )
    ]
    for fetch in fetches:
        fetch.start()
    fetches[0].wait()

    low_lanes = iota((16, 128), 1) < 64
    for pair in range(NC // 2):
        first = pool_ref[0:16, pair * 128 : pair * 128 + 128].astype(F32)
        second = pool_ref[16:32, pair * 128 : pair * 128 + 128].astype(F32)
        bags_send[2 * pair] = jnp.where(low_lanes, first, pltpu.roll(second, 64, 1)).astype(BF16)
        bags_send[2 * pair + 1] = jnp.where(low_lanes, pltpu.roll(first, 64, 1), second).astype(BF16)
    bags_recv[col] = bags_send[col]
    pl.semaphore_wait(barrier, NC + NY + NZ - 3)
    start(0, NC, along_col, col, bags_send, bags_recv)

    for fetch in fetches[1:6]:
        fetch.wait()
    owner = owner_ref[...].reshape(1, LK)
    target = iota((NY * NZ, LK), 0) == owner
    earlier = one_hot(iota((LK, LK), 0) < iota((LK, LK), 1))
    before = dot(one_hot(target), earlier)
    rank = jnp.sum(jnp.where(target, before, 0.0), axis=0, keepdims=True).astype(jnp.int32)
    owner_z, owner_y = owner >> 3, owner & 7
    half, quarter = rank >> 2, rank & 3
    table_row = row_ref[...].reshape(1, LK)
    line = owner_y * (2 * NZ) + owner_z * 2 + half
    lane = lax.rem(z, 4) * 32 + y * 4 + quarter
    in_lane = iota((128, LK), 0) == lane
    high = jnp.where(in_lane, (table_row >> 8) + 1, 0).astype(F32).astype(BF16)
    low = jnp.where(in_lane, table_row & 255, 0).astype(F32).astype(BF16)
    in_line = one_hot(iota((NY * NZ * 2, LK), 0) == line)
    codes = dot_t(in_line, high) * 256.0 + dot_t(in_line, low)
    rows_y_send[...] = codes.reshape(NY, 2 * NZ, 128)
    rows_y_recv[y] = rows_y_send[y]
    start(1, NY, along_y, y, rows_y_send, rows_y_recv)

    def place_of_bag(bag):
        return ((bag >> 4) & 1) * 128 + (bag >> 5) * 16 + (bag & 15)

    position = owner_y * (NZ * 4) + owner_z * 4 + quarter + half * LK
    placed = one_hot(iota((2 * LK, LK), 0) == position)
    cold_place = place_of_bag(bag_ref[...].reshape(1, LK)) + 1
    cold_place = jnp.broadcast_to(cold_place, (8, LK)).astype(F32).astype(BF16)
    slot_place = dot_t(placed, cold_place)[:, 0:1].astype(jnp.int32)
    bag_number = iota((LK, 256), 1) + 1
    pick = jnp.concatenate(
        [one_hot(slot_place[:LK] == bag_number), one_hot(slot_place[LK:] == bag_number)], axis=1
    )

    hot_id = hot_id_ref[...].reshape(1, LH)
    hot_line = (hot_id >> 4) * 8 + (hot_id & 7) + ((hot_id >> 3) & 1) * (NZ * 8)
    hot_rows = one_hot(iota((NZ * 16, LH), 0) == hot_line)
    hot_place = place_of_bag(hot_bag_ref[...].reshape(1, LH))
    counts = dot_t(hot_rows, one_hot(iota((256, LH), 0) == hot_place))
    counts = jnp.concatenate([counts[: NZ * 8], counts[NZ * 8 :]], axis=1)
    count_high = counts.astype(BF16)
    count_low = (counts - count_high.astype(F32)).astype(BF16)

    wait(recv_sems.at[0], NC, bags_recv)
    bags = bags_recv[...].reshape(128, 128).astype(F32)
    rolled = pltpu.roll(bags, 64, 1)
    left = iota((128, 128), 1) < 64
    spread = jnp.concatenate(
        [
            jnp.where(left, bags, 0.0),
            jnp.where(left, rolled, 0.0),
            jnp.where(left, 0.0, rolled),
            jnp.where(left, 0.0, bags),
        ],
        axis=0,
    ).astype(BF16)
    cold_y_send[...] = dot(pick, spread).astype(BF16).reshape(NY, NZ * 4, 128)
    cold_y_recv[y] = cold_y_send[y]
    start(2, NY, along_y, y, cold_y_send, cold_y_recv)
    hot_z_send[...] = (dot(count_high, spread) + dot(count_low, spread)).reshape(NZ, 8, 128)
    hot_z_recv[z] = hot_z_send[z]
    start(3, NZ, along_z, z, hot_z_send, hot_z_recv)

    wait(recv_sems.at[1], NY, rows_y_recv)
    merged = jnp.sum(rows_y_recv[...], axis=0)
    for other in range(NZ):
        rows_z_send[other, 0:2] = merged[2 * other : 2 * other + 2]
        rows_z_send[other, 2:8] = jnp.zeros((6, 128), F32)
    rows_z_recv[z] = rows_z_send[z]
    start(4, NZ, along_z, z, rows_z_send, rows_z_recv)

    out_row = iota((LK, LK), 0)
    source = ((out_row >> 2) & 7) * (NZ * 4) + (out_row >> 5) * 4 + (out_row & 3)
    regroup = one_hot(iota((LK, LK), 1) == source)

    wait(recv_sems.at[2], NY, cold_y_recv)
    regrouped = dot(regroup, cold_y_recv[...].reshape(LK, 128)).astype(BF16)
    cold_z_send[...] = regrouped.reshape(NZ, 32, 128)
    cold_z_recv[z] = cold_z_send[z]
    start(5, NZ, along_z, z, cold_z_send, cold_z_recv)

    wait(recv_sems.at[3], NZ, hot_z_recv)
    hot_y_recv[y] = jnp.sum(hot_z_recv[...], axis=0)
    start(6, NY, along_y, y, hot_y_recv, hot_y_recv)

    wait(recv_sems.at[4], NZ, rows_z_recv)
    code = jnp.concatenate(
        [jnp.sum(rows_z_recv[4 * g : 4 * g + 4], axis=0) for g in range(NZ // 4)], axis=1
    ).astype(jnp.int32)
    code_high, code_low = code >> 8, code & 255
    low_number = iota((256, LK), 0)
    land = [one_hot(code_low[side : side + 1] == low_number) for side in range(2)]

    wait(recv_sems.at[6], NY, hot_y_recv)
    hot_all_recv[z] = jnp.sum(hot_y_recv[...], axis=0)
    start(7, NZ, along_z, z, hot_all_recv, hot_all_recv)

    wait(recv_sems.at[5], NZ, cold_z_recv)
    arrived = cold_z_recv[...].reshape(LK, 128).astype(F32).T
    grads = jnp.zeros((512, 256), F32)
    for side in range(2):
        mine = arrived[64 * side : 64 * side + 64]
        masked = jnp.concatenate(
            [jnp.where(code_high[side : side + 1] == h + 1, mine, 0.0) for h in range(8)], axis=0
        ).astype(BF16)
        grads += dot_t(masked, land[side])
    squares = []
    for h in range(8):
        part = grads[64 * h : 64 * h + 64]
        grad_ref[:, 256 * h : 256 * h + 256] = part
        squares.append(jnp.sum(part * part, axis=0, keepdims=True))
    square_recv[col, :, 0:256] = jnp.concatenate(squares, axis=0)

    wait(recv_sems.at[7], NZ, hot_all_recv)
    pieces = []
    for other in range(NZ):
        piece = hot_all_recv[other]
        pieces += [piece, pltpu.roll(piece, 64, 1)]
    hot_grad = jnp.concatenate(pieces + [jnp.zeros((64, 128), F32)], axis=0).T[0:64]
    hot_squares = jnp.sum(hot_grad * hot_grad, axis=0, keepdims=True)
    square_recv[col, :, 256:384] = jnp.concatenate(
        [hot_squares[:, 0:128], hot_squares[:, 128:256], jnp.zeros((6, 128), F32)], axis=0
    )
    start(8, NC, along_col, col, square_recv, square_recv)
    for fetch in fetches[6:]:
        fetch.wait()
    wait(recv_sems.at[8], NC, square_recv)
    total = square_recv[0]
    for other in range(1, NC):
        total += square_recv[other]
    stores = []

    def store(source, target):
        copy = pltpu.make_async_copy(source, target, store_sems.at[len(stores)])
        copy.start()
        stores.append(copy)

    hot_total = jnp.concatenate([total[0:1, 256:384], total[1:2, 256:320]], axis=1)
    accum = hot_accum_ref[...].reshape(1, 192) + hot_total / E
    new_hot_accum_ref[...] = accum.reshape(192)
    store(new_hot_accum_ref, new_hot_accum_hbm)
    new_hot_ref[...] = hot_table_ref[...] - hot_grad[:, 0:192] * (LR / (jnp.sqrt(accum) + EPS))
    store(new_hot_ref, new_hot_hbm)
    for h in range(8):
        at = slice(256 * h, 256 * h + 256)
        accum = accum_ref[at].reshape(1, 256) + total[h : h + 1, 0:256] / E
        new_accum_ref[at] = accum.reshape(256)
        scale = LR / (jnp.sqrt(accum) + EPS)
        new_ref[:, at] = table_ref[:, at] - grad_ref[:, at] * scale
        if h % 2 == 1:
            done = slice(256 * h - 256, 256 * h + 256)
            store(new_ref.at[:, done], new_hbm.at[:, done])
    store(new_accum_ref, new_accum_hbm)

    for stage, count, send in (
        (0, NC, bags_send),
        (1, NY, rows_y_send),
        (2, NY, cold_y_send),
        (3, NZ, hot_z_send),
        (4, NZ, rows_z_send),
        (5, NZ, cold_z_send),
        (6, NY, hot_y_recv),
        (7, NZ, hot_all_recv),
        (8, NC, square_recv),
    ):
        wait(send_sems.at[stage], count, send)
    for copy in stores:
        copy.wait()


def exchange(*operands):
    hbm = pl.BlockSpec(memory_space=pltpu.HBM)
    return pl.pallas_call(
        exchange_kernel,
        out_shape=tuple(jax.ShapeDtypeStruct(a.shape, F32) for a in operands[6:]),
        in_specs=[hbm] * 10,
        out_specs=(hbm,) * 4,
        scratch_shapes=[
            *(pltpu.VMEM(a.shape, a.dtype) for a in operands),
            *(pltpu.VMEM(a.shape, F32) for a in operands[6:]),
            pltpu.VMEM((64, 2048), F32),
            pltpu.VMEM((NC, 16, 128), BF16),
            pltpu.VMEM((NC, 16, 128), BF16),
            pltpu.VMEM((NY, 2 * NZ, 128), F32),
            pltpu.VMEM((NY, 2 * NZ, 128), F32),
            pltpu.VMEM((NZ, 8, 128), F32),
            pltpu.VMEM((NZ, 8, 128), F32),
            pltpu.VMEM((NY, NZ * 4, 128), BF16),
            pltpu.VMEM((NY, NZ * 4, 128), BF16),
            pltpu.VMEM((NZ, 32, 128), BF16),
            pltpu.VMEM((NZ, 32, 128), BF16),
            pltpu.VMEM((NZ, 8, 128), F32),
            pltpu.VMEM((NZ, 8, 128), F32),
            pltpu.VMEM((NY, 8, 128), F32),
            pltpu.VMEM((NZ, 8, 128), F32),
            pltpu.VMEM((NC, 8, 384), F32),
            pltpu.SemaphoreType.DMA((10,)),
            pltpu.SemaphoreType.DMA((7,)),
            pltpu.SemaphoreType.DMA((9,)),
            pltpu.SemaphoreType.DMA((9,)),
        ],
        compiler_params=pltpu.CompilerParams(
            collective_id=0, has_side_effects=True, vmem_limit_bytes=60 * 1024 * 1024
        ),
        name="exchange",
    )(*operands)


def write_kernel(table, accum, hot_table, hot_accum, *refs):
    sems = refs[4]
    copies = [
        (table.at[0:32], refs[0].at[0:32]),
        (table.at[32:64], refs[0].at[32:64]),
        (accum, refs[1]),
        (hot_table, refs[2]),
        (hot_accum, refs[3]),
    ]
    copies = [pltpu.make_async_copy(*pair, sems.at[i]) for i, pair in enumerate(copies)]
    for copy in copies:
        copy.start()
    for copy in copies:
        copy.wait()


def write(*arrays):
    hbm = pl.BlockSpec(memory_space=pltpu.HBM)
    return pl.pallas_call(
        write_kernel,
        out_shape=tuple(jax.ShapeDtypeStruct(a.shape, a.dtype) for a in arrays),
        in_specs=[hbm] * 4,
        out_specs=(hbm,) * 4,
        scratch_shapes=[pltpu.SemaphoreType.DMA((5,))],
        compiler_params=pltpu.CompilerParams(vmem_limit_bytes=60 * 1024 * 1024),
        name="write",
    )(*arrays)


def on_device(
    pooled_grad,
    cold_table,
    cold_accum,
    hot_table,
    hot_accum,
    cold_owner,
    cold_row,
    cold_bag,
    hot_id,
    hot_bag,
):
    updated = exchange(
        pooled_grad.reshape(32, E),
        cold_owner.T,
        cold_row,
        cold_bag,
        hot_id,
        hot_bag,
        cold_table,
        cold_accum,
        hot_table,
        hot_accum,
    )
    return tuple(write(*updated))


def solution(mesh):
    in_specs = (
        P(("row", "col"), None, None),
        P("col", "row"),
        P("row"),
        P("col", None),
        P(),
        P("row", None),
        P("row"),
        P("row"),
        P("row"),
        P("row"),
    )
    out_specs = (P("col", "row"), P("row"), P("col", None), P())
    return jax.shard_map(
        on_device, mesh=mesh, in_specs=in_specs, out_specs=out_specs, check_vma=False
    )
```

```python
import jax
import jax.numpy as jnp
from jax import lax
from jax.experimental import pallas as pl
from jax.experimental.pallas import tpu as pltpu
from jax.sharding import PartitionSpec as P

E = 512
LR = 0.3
EPS = 1e-08
MESH = pl.DeviceIdType.MESH

NC = 8
NY = 8
NZ = 12
LK = 384
LH = 512
CAP = 8
F32 = jnp.float32
BF16 = jnp.bfloat16


def iota(shape, dim):
    return lax.broadcasted_iota(jnp.int32, shape, dim)


def one_hot(mask):
    return jnp.where(mask, 1.0, 0.0).astype(BF16)


def dot(a, b):
    return jnp.dot(a, b, preferred_element_type=F32)


def dot_t(a, b):
    return lax.dot_general(a, b, (((1,), (1,)), ((), ())), preferred_element_type=F32)


def exchange_kernel(
    pool_hbm,
    owner_hbm,
    row_hbm,
    bag_hbm,
    hot_id_hbm,
    hot_bag_hbm,
    table_hbm,
    accum_hbm,
    hot_table_hbm,
    hot_accum_hbm,
    new_hbm,
    new_accum_hbm,
    new_hot_hbm,
    new_hot_accum_hbm,
    pool_ref,
    owner_ref,
    row_ref,
    bag_ref,
    hot_id_ref,
    hot_bag_ref,
    table_ref,
    accum_ref,
    hot_table_ref,
    hot_accum_ref,
    new_ref,
    new_accum_ref,
    new_hot_ref,
    new_hot_accum_ref,
    grad_ref,
    bags_send,
    bags_recv,
    rows_y_send,
    rows_y_recv,
    rows_z_send,
    rows_z_recv,
    cold_y_send,
    cold_y_recv,
    cold_z_send,
    cold_z_recv,
    hot_z_send,
    hot_z_recv,
    hot_y_recv,
    hot_all_recv,
    square_recv,
    hot_square_recv,
    fetch_sems,
    store_sems,
    send_sems,
    recv_sems,
):
    row = lax.axis_index("row")
    col = lax.axis_index("col")
    z = lax.div(row, NY)
    y = lax.rem(row, NY)

    def along_col(k):
        other = lax.rem(col + k, NC)
        return other, {"row": row, "col": other}

    def along_y(k):
        other = lax.rem(y + k, NY)
        return other, {"row": z * NY + other, "col": col}

    def along_z(k):
        other = lax.rem(z + k, NZ)
        return other, {"row": other * NY + y, "col": col}

    def start(stage, count, along, me, send, recv):
        for k in sorted(range(1, count), key=lambda k: -min(k, count - k)):
            other, device = along(k)
            pltpu.make_async_remote_copy(
                src_ref=send.at[me if send is recv else other],
                dst_ref=recv.at[me],
                send_sem=send_sems.at[stage],
                recv_sem=recv_sems.at[stage],
                device_id=device,
                device_id_type=MESH,
            ).start()

    def wait(sem, count, ref):
        part = ref.at[pl.ds(0, count - 1)]
        pltpu.make_async_copy(part, part, sem).wait()

    barrier = pltpu.get_barrier_semaphore()
    for count, along in ((NC, along_col), (NY, along_y), (NZ, along_z)):
        for k in range(1, count):
            pl.semaphore_signal(barrier, inc=1, device_id=along(k)[1], device_id_type=MESH)

    fetches = [
        pltpu.make_async_copy(source, target, fetch_sems.at[i])
        for i, (source, target) in enumerate(
            (
                (pool_hbm, pool_ref),
                (owner_hbm, owner_ref),
                (row_hbm, row_ref),
                (bag_hbm, bag_ref),
                (hot_id_hbm, hot_id_ref),
                (hot_bag_hbm, hot_bag_ref),
                (table_hbm, table_ref),
                (accum_hbm, accum_ref),
                (hot_table_hbm, hot_table_ref),
                (hot_accum_hbm, hot_accum_ref),
            )
        )
    ]
    for fetch in fetches:
        fetch.start()
    fetches[0].wait()

    low_lanes = iota((16, 128), 1) < 64
    for pair in range(NC // 2):
        first = pool_ref[0:16, pair * 128 : pair * 128 + 128].astype(F32)
        second = pool_ref[16:32, pair * 128 : pair * 128 + 128].astype(F32)
        bags_send[2 * pair] = jnp.where(low_lanes, first, pltpu.roll(second, 64, 1)).astype(BF16)
        bags_send[2 * pair + 1] = jnp.where(low_lanes, pltpu.roll(first, 64, 1), second).astype(BF16)
    bags_recv[col] = bags_send[col]
    pl.semaphore_wait(barrier, NC + NY + NZ - 3)
    start(0, NC, along_col, col, bags_send, bags_recv)

    def place_of_bag(bag):
        return ((bag >> 4) & 1) * 128 + (bag >> 5) * 16 + (bag & 15)

    for fetch in fetches[1:6]:
        fetch.wait()
    hot_id = hot_id_ref[...].reshape(1, LH)
    hot_line = (hot_id >> 4) * 8 + (hot_id & 7) + ((hot_id >> 3) & 1) * (NZ * 8)
    hot_rows = one_hot(iota((NZ * 16, LH), 0) == hot_line)
    hot_place = place_of_bag(hot_bag_ref[...].reshape(1, LH))
    counts = dot_t(hot_rows, one_hot(iota((256, LH), 0) == hot_place))
    counts = jnp.concatenate([counts[: NZ * 8], counts[NZ * 8 :]], axis=1)
    count_high = counts.astype(BF16)
    count_low = (counts - count_high.astype(F32)).astype(BF16)

    owner = owner_ref[...].reshape(1, LK)
    target = iota((NY * NZ, LK), 0) == owner
    taken = one_hot(target)
    earlier = one_hot(iota((128, 128), 0) < iota((128, 128), 1))
    carry = jnp.zeros((NY * NZ, 1), F32)
    ranks = []
    for part in range(LK // 128):
        at = slice(128 * part, 128 * part + 128)
        before = dot(taken[:, at], earlier) + carry
        ranks.append(jnp.sum(jnp.where(target[:, at], before, 0.0), axis=0, keepdims=True))
        carry += jnp.sum(jnp.where(target[:, at], 1.0, 0.0), axis=1, keepdims=True)
    rank = jnp.concatenate(ranks, axis=1).astype(jnp.int32)
    owner_z, owner_y = owner >> 3, owner & 7
    half, quarter = rank >> 2, rank & 3
    table_row = row_ref[...].reshape(1, LK)
    line = owner_y * (2 * NZ) + owner_z * 2 + half
    lane = lax.rem(z, 4) * 32 + y * 4 + quarter
    in_lane = iota((128, LK), 0) == lane
    high = jnp.where(in_lane, (table_row >> 8) + 1, 0).astype(F32).astype(BF16)
    low = jnp.where(in_lane, table_row & 255, 0).astype(F32).astype(BF16)
    in_line = one_hot(iota((NY * NZ * 2, LK), 0) == line)
    codes = dot_t(in_line, high) * 256.0 + dot_t(in_line, low)
    rows_y_send[...] = codes.reshape(NY, 2 * NZ, 128)
    rows_y_recv[y] = rows_y_send[y]
    start(1, NY, along_y, y, rows_y_send, rows_y_recv)

    spot = one_hot(iota((NY * NZ, LK), 0) == half * (NZ * 4) + owner_z * 4 + quarter)
    cold_place = place_of_bag(bag_ref[...].reshape(1, LK)) + 1
    weight = jnp.where(iota((NY, LK), 0) == owner_y, cold_place, 0).astype(F32).astype(BF16)
    slot_place = dot_t(spot, weight).astype(jnp.int32)
    bag_number = iota((NY * NZ, 256), 1) + 1
    picks = []
    for other in range(NY):
        pick = jnp.where(slot_place[:, other : other + 1] == bag_number, 1.0, 0.0)
        picks.append(jnp.concatenate([pick[: NZ * 4], pick[NZ * 4 :]], axis=1))
    pick = jnp.concatenate(picks, axis=0).astype(BF16)

    wait(recv_sems.at[0], NC, bags_recv)
    bags = bags_recv[...].reshape(128, 128).astype(F32)
    rolled = pltpu.roll(bags, 64, 1)
    left = iota((128, 128), 1) < 64
    spread = jnp.concatenate(
        [
            jnp.where(left, bags, 0.0),
            jnp.where(left, rolled, 0.0),
            jnp.where(left, 0.0, rolled),
            jnp.where(left, 0.0, bags),
        ],
        axis=0,
    ).astype(BF16)
    hot_z_send[...] = (dot(count_high, spread) + dot(count_low, spread)).reshape(NZ, 8, 128)
    hot_z_recv[z] = hot_z_send[z]
    start(3, NZ, along_z, z, hot_z_send, hot_z_recv)
    cold_y_send[...] = dot(pick, spread).astype(BF16).reshape(NY, NZ * 4, 128)
    cold_y_recv[y] = cold_y_send[y]
    start(2, NY, along_y, y, cold_y_send, cold_y_recv)

    wait(recv_sems.at[1], NY, rows_y_recv)
    merged = jnp.sum(rows_y_recv[...], axis=0)
    for other in range(NZ):
        rows_z_send[other, 0:2] = merged[2 * other : 2 * other + 2]
        rows_z_send[other, 2:8] = jnp.zeros((6, 128), F32)
    rows_z_recv[z] = rows_z_send[z]
    start(4, NZ, along_z, z, rows_z_send, rows_z_recv)

    out_row = iota((LK, LK), 0)
    source = ((out_row >> 2) & 7) * (NZ * 4) + (out_row >> 5) * 4 + (out_row & 3)
    regroup = one_hot(iota((LK, LK), 1) == source)

    wait(recv_sems.at[3], NZ, hot_z_recv)
    hot_y_recv[y] = jnp.sum(hot_z_recv[...], axis=0)
    start(6, NY, along_y, y, hot_y_recv, hot_y_recv)

    wait(recv_sems.at[2], NY, cold_y_recv)
    regrouped = dot(regroup, cold_y_recv[...].reshape(LK, 128)).astype(BF16)
    cold_z_send[...] = regrouped.reshape(NZ, 32, 128)
    cold_z_recv[z] = cold_z_send[z]
    start(5, NZ, along_z, z, cold_z_send, cold_z_recv)

    wait(recv_sems.at[4], NZ, rows_z_recv)
    code = jnp.concatenate(
        [jnp.sum(rows_z_recv[4 * g : 4 * g + 4], axis=0) for g in range(NZ // 4)], axis=1
    ).astype(jnp.int32)
    code_high, code_low = code >> 8, code & 255
    low_number = iota((256, LK), 0)
    land = [one_hot(code_low[side : side + 1] == low_number) for side in range(2)]

    wait(recv_sems.at[6], NY, hot_y_recv)
    hot_all_recv[z] = jnp.sum(hot_y_recv[...], axis=0)
    start(7, NZ, along_z, z, hot_all_recv, hot_all_recv)

    wait(recv_sems.at[5], NZ, cold_z_recv)
    arrived = cold_z_recv[...].reshape(LK, 128).astype(F32).T
    grads = jnp.zeros((512, 256), F32)
    for side in range(2):
        mine = arrived[64 * side : 64 * side + 64]
        masked = jnp.concatenate(
            [jnp.where(code_high[side : side + 1] == h + 1, mine, 0.0) for h in range(8)], axis=0
        ).astype(BF16)
        grads += dot_t(masked, land[side])
    squares = []
    for h in range(8):
        part = grads[64 * h : 64 * h + 64]
        grad_ref[:, 256 * h : 256 * h + 256] = part
        squares.append(jnp.sum(part * part, axis=0, keepdims=True))
    square_recv[col] = jnp.concatenate(squares, axis=0)
    start(8, NC, along_col, col, square_recv, square_recv)

    wait(recv_sems.at[7], NZ, hot_all_recv)
    pieces = []
    for other in range(NZ):
        piece = hot_all_recv[other]
        pieces += [piece, pltpu.roll(piece, 64, 1)]
    hot_grad = jnp.concatenate(pieces + [jnp.zeros((64, 128), F32)], axis=0).T[0:64]
    hot_squares = jnp.sum(hot_grad * hot_grad, axis=0, keepdims=True)
    hot_square_recv[col] = jnp.concatenate(
        [hot_squares[:, 0:128], hot_squares[:, 128:256], jnp.zeros((6, 128), F32)], axis=0
    )
    start(9, NC, along_col, col, hot_square_recv, hot_square_recv)
    for fetch in fetches[6:]:
        fetch.wait()

    stores = []

    def store(source, target):
        copy = pltpu.make_async_copy(source, target, store_sems.at[len(stores)])
        copy.start()
        stores.append(copy)

    def summed(ref):
        total = ref[0]
        for other in range(1, NC):
            total += ref[other]
        return total

    wait(recv_sems.at[8], NC, square_recv)
    total = summed(square_recv)
    for h in range(8):
        at = slice(256 * h, 256 * h + 256)
        accum = accum_ref[at].reshape(1, 256) + total[h : h + 1] / E
        new_accum_ref[at] = accum.reshape(256)
        scale = LR / (jnp.sqrt(accum) + EPS)
        new_ref[:, at] = table_ref[:, at] - grad_ref[:, at] * scale
        if h % 2 == 1:
            done = slice(256 * h - 256, 256 * h + 256)
            store(new_ref.at[:, done], new_hbm.at[:, done])
    store(new_accum_ref, new_accum_hbm)

    wait(recv_sems.at[9], NC, hot_square_recv)
    total = summed(hot_square_recv)
    hot_total = jnp.concatenate([total[0:1], total[1:2, 0:64]], axis=1)
    accum = hot_accum_ref[...].reshape(1, 192) + hot_total / E
    new_hot_accum_ref[...] = accum.reshape(192)
    store(new_hot_accum_ref, new_hot_accum_hbm)
    new_hot_ref[...] = hot_table_ref[...] - hot_grad[:, 0:192] * (LR / (jnp.sqrt(accum) + EPS))
    store(new_hot_ref, new_hot_hbm)

    for stage, count, send in (
        (0, NC, bags_send),
        (1, NY, rows_y_send),
        (2, NY, cold_y_send),
        (3, NZ, hot_z_send),
        (4, NZ, rows_z_send),
        (5, NZ, cold_z_send),
        (6, NY, hot_y_recv),
        (7, NZ, hot_all_recv),
        (8, NC, square_recv),
        (9, NC, hot_square_recv),
    ):
        wait(send_sems.at[stage], count, send)
    for copy in stores:
        copy.wait()


def exchange(*operands):
    hbm = pl.BlockSpec(memory_space=pltpu.HBM)
    return pl.pallas_call(
        exchange_kernel,
        out_shape=tuple(jax.ShapeDtypeStruct(a.shape, F32) for a in operands[6:]),
        in_specs=[hbm] * 10,
        out_specs=(hbm,) * 4,
        scratch_shapes=[
            *(pltpu.VMEM(a.shape, a.dtype) for a in operands),
            *(pltpu.VMEM(a.shape, F32) for a in operands[6:]),
            pltpu.VMEM((64, 2048), F32),
            pltpu.VMEM((NC, 16, 128), BF16),
            pltpu.VMEM((NC, 16, 128), BF16),
            pltpu.VMEM((NY, 2 * NZ, 128), F32),
            pltpu.VMEM((NY, 2 * NZ, 128), F32),
            pltpu.VMEM((NZ, 8, 128), F32),
            pltpu.VMEM((NZ, 8, 128), F32),
            pltpu.VMEM((NY, NZ * 4, 128), BF16),
            pltpu.VMEM((NY, NZ * 4, 128), BF16),
            pltpu.VMEM((NZ, 32, 128), BF16),
            pltpu.VMEM((NZ, 32, 128), BF16),
            pltpu.VMEM((NZ, 8, 128), F32),
            pltpu.VMEM((NZ, 8, 128), F32),
            pltpu.VMEM((NY, 8, 128), F32),
            pltpu.VMEM((NZ, 8, 128), F32),
            pltpu.VMEM((NC, 8, 256), F32),
            pltpu.VMEM((NC, 8, 128), F32),
            pltpu.SemaphoreType.DMA((10,)),
            pltpu.SemaphoreType.DMA((7,)),
            pltpu.SemaphoreType.DMA((10,)),
            pltpu.SemaphoreType.DMA((10,)),
        ],
        compiler_params=pltpu.CompilerParams(
            collective_id=0, has_side_effects=True, vmem_limit_bytes=60 * 1024 * 1024
        ),
        name="exchange",
    )(*operands)


def write_kernel(*refs):
    sources, targets, holds, sems = refs[0:4], refs[4:8], refs[8:12], refs[12]
    rows = sources[0].shape[0] // 4
    parts = [(0, pl.ds(rows * part, rows)) for part in range(4)]
    parts += [(i, slice(None)) for i in range(1, 4)]
    loads, stores = [], []
    for n, (i, at) in enumerate(parts):
        loads.append(pltpu.make_async_copy(sources[i].at[at], holds[i].at[at], sems.at[0, n]))
        stores.append(pltpu.make_async_copy(holds[i].at[at], targets[i].at[at], sems.at[1, n]))
    for load in loads:
        load.start()
    for load, store in zip(loads, stores):
        load.wait()
        store.start()
    for store in stores:
        store.wait()


def write(*arrays):
    hbm = pl.BlockSpec(memory_space=pltpu.HBM)
    return pl.pallas_call(
        write_kernel,
        out_shape=tuple(jax.ShapeDtypeStruct(a.shape, a.dtype) for a in arrays),
        in_specs=[hbm] * 4,
        out_specs=(hbm,) * 4,
        scratch_shapes=[
            *(pltpu.VMEM(a.shape, a.dtype) for a in arrays),
            pltpu.SemaphoreType.DMA((2, 7)),
        ],
        compiler_params=pltpu.CompilerParams(vmem_limit_bytes=60 * 1024 * 1024),
        name="write",
    )(*arrays)


def on_device(
    pooled_grad,
    cold_table,
    cold_accum,
    hot_table,
    hot_accum,
    cold_owner,
    cold_row,
    cold_bag,
    hot_id,
    hot_bag,
):
    updated = exchange(
        pooled_grad.reshape(32, E),
        cold_owner.T,
        cold_row,
        cold_bag,
        hot_id,
        hot_bag,
        cold_table,
        cold_accum,
        hot_table,
        hot_accum,
    )
    return tuple(write(*updated))


def solution(mesh):
    in_specs = (
        P(("row", "col"), None, None),
        P("col", "row"),
        P("row"),
        P("col", None),
        P(),
        P("row", None),
        P("row"),
        P("row"),
        P("row"),
        P("row"),
    )
    out_specs = (P("col", "row"), P("row"), P("col", None), P())
    return jax.shard_map(
        on_device, mesh=mesh, in_specs=in_specs, out_specs=out_specs, check_vma=False
    )
```

```python
import jax
import jax.numpy as jnp
from jax import lax
from jax.experimental import pallas as pl
from jax.experimental.pallas import tpu as pltpu
from jax.sharding import PartitionSpec as P

E = 512
LR = 0.3
EPS = 1e-08
MESH = pl.DeviceIdType.MESH

NC = 8
NY = 8
NZ = 12
LK = 384
LH = 512
CAP = 8
F32 = jnp.float32
BF16 = jnp.bfloat16


def iota(shape, dim):
    return lax.broadcasted_iota(jnp.int32, shape, dim)


def one_hot(mask):
    return jnp.where(mask, 1.0, 0.0).astype(BF16)


def dot(a, b):
    return jnp.dot(a, b, preferred_element_type=F32)


def dot_t(a, b):
    return lax.dot_general(a, b, (((1,), (1,)), ((), ())), preferred_element_type=F32)


def exchange_kernel(
    pool_hbm,
    owner_hbm,
    row_hbm,
    bag_hbm,
    hot_id_hbm,
    hot_bag_hbm,
    table_hbm,
    accum_hbm,
    hot_table_hbm,
    hot_accum_hbm,
    new_hbm,
    new_accum_hbm,
    new_hot_hbm,
    new_hot_accum_hbm,
    pool_ref,
    owner_ref,
    row_ref,
    bag_ref,
    hot_id_ref,
    hot_bag_ref,
    table_ref,
    accum_ref,
    hot_table_ref,
    hot_accum_ref,
    new_ref,
    new_accum_ref,
    new_hot_ref,
    new_hot_accum_ref,
    grad_ref,
    bags_send,
    bags_recv,
    rows_y_send,
    rows_y_recv,
    rows_z_send,
    rows_z_recv,
    cold_send,
    cold_recv,
    hot_z_send,
    hot_z_recv,
    hot_y_recv,
    hot_all_recv,
    square_recv,
    hot_square_recv,
    hot_total_recv,
    fetch_sems,
    store_sems,
    send_sems,
    recv_sems,
):
    row = lax.axis_index("row")
    col = lax.axis_index("col")
    z = lax.div(row, NY)
    y = lax.rem(row, NY)

    def along_col(k):
        other = lax.rem(col + k, NC)
        return other, {"row": row, "col": other}

    def along_y(k):
        other = lax.rem(y + k, NY)
        return other, {"row": z * NY + other, "col": col}

    def along_z(k):
        other = lax.rem(z + k, NZ)
        return other, {"row": other * NY + y, "col": col}

    def start(stage, count, along, me, send, recv):
        for k in sorted(range(1, count), key=lambda k: -min(k, count - k)):
            other, device = along(k)
            pltpu.make_async_remote_copy(
                src_ref=send.at[me if send is recv else other],
                dst_ref=recv.at[me],
                send_sem=send_sems.at[stage],
                recv_sem=recv_sems.at[stage],
                device_id=device,
                device_id_type=MESH,
            ).start()

    def wait(sem, count, ref):
        part = ref.at[pl.ds(0, count - 1)]
        pltpu.make_async_copy(part, part, sem).wait()

    fetches = [
        pltpu.make_async_copy(source, target, fetch_sems.at[i])
        for i, (source, target) in enumerate(
            (
                (pool_hbm, pool_ref),
                (owner_hbm, owner_ref),
                (row_hbm, row_ref),
                (bag_hbm, bag_ref),
                (hot_id_hbm, hot_id_ref),
                (hot_bag_hbm, hot_bag_ref),
                (table_hbm, table_ref),
                (accum_hbm, accum_ref),
                (hot_table_hbm, hot_table_ref),
                (hot_accum_hbm, hot_accum_ref),
            )
        )
    ]
    for fetch in fetches:
        fetch.start()
    barrier = pltpu.get_barrier_semaphore()
    for count, along in ((NC, along_col), (NY, along_y), (NZ, along_z)):
        for k in range(1, count):
            pl.semaphore_signal(barrier, inc=1, device_id=along(k)[1], device_id_type=MESH)

    def around(step_z, step_y):
        other = lax.rem(z + step_z, NZ) * NY + lax.rem(y + step_y, NY)
        return other, {"row": other, "col": col}

    def all_of_row(act):
        def ring(i, carry):
            step_z = NZ // 2 + (1 - 2 * lax.rem(i, 2)) * lax.div(i + 1, 2)
            for step_y in (4, 3, 5, 2, 6, 1, 7, 0):
                act(*around(step_z, step_y))
            return carry

        lax.fori_loop(0, NZ - 1, ring, 0)
        for step_y in (4, 3, 5, 2, 6, 1, 7):
            act(*around(0, step_y))

    fetches[0].wait()

    low_lanes = iota((16, 128), 1) < 64
    for pair in range(NC // 2):
        first = pool_ref[0:16, pair * 128 : pair * 128 + 128].astype(F32)
        second = pool_ref[16:32, pair * 128 : pair * 128 + 128].astype(F32)
        bags_send[2 * pair] = jnp.where(low_lanes, first, pltpu.roll(second, 64, 1)).astype(BF16)
        bags_send[2 * pair + 1] = jnp.where(low_lanes, pltpu.roll(first, 64, 1), second).astype(BF16)
    bags_recv[col] = bags_send[col]
    pl.semaphore_wait(barrier, NC + NY + NZ - 3)
    start(0, NC, along_col, col, bags_send, bags_recv)

    def place_of_bag(bag):
        return ((bag >> 4) & 1) * 128 + (bag >> 5) * 16 + (bag & 15)

    for fetch in fetches[1:6]:
        fetch.wait()
    hot_id = hot_id_ref[...].reshape(1, LH)
    hot_line = (hot_id >> 4) * 8 + (hot_id & 7) + ((hot_id >> 3) & 1) * (NZ * 8)
    hot_rows = one_hot(iota((NZ * 16, LH), 0) == hot_line)
    hot_place = place_of_bag(hot_bag_ref[...].reshape(1, LH))
    counts = dot_t(hot_rows, one_hot(iota((256, LH), 0) == hot_place))
    counts = jnp.concatenate([counts[: NZ * 8], counts[NZ * 8 :]], axis=1)
    count_high = counts.astype(BF16)
    count_low = (counts - count_high.astype(F32)).astype(BF16)
    count_parts = jnp.concatenate([count_high, count_low], axis=0)

    owner = owner_ref[...].reshape(1, LK)
    target = iota((NY * NZ, LK), 0) == owner
    taken = one_hot(target)
    earlier = one_hot(iota((128, 128), 0) < iota((128, 128), 1))
    carry = jnp.zeros((NY * NZ, 1), F32)
    ranks = []
    for part in range(LK // 128):
        at = slice(128 * part, 128 * part + 128)
        before = dot(taken[:, at], earlier) + carry
        ranks.append(jnp.sum(jnp.where(target[:, at], before, 0.0), axis=0, keepdims=True))
        carry += jnp.sum(jnp.where(target[:, at], 1.0, 0.0), axis=1, keepdims=True)
    rank = jnp.concatenate(ranks, axis=1).astype(jnp.int32)
    owner_z, owner_y = owner >> 3, owner & 7
    half, quarter = rank >> 2, rank & 3
    table_row = row_ref[...].reshape(1, LK)
    line = owner_y * (2 * NZ) + owner_z * 2 + half
    lane = lax.rem(z, 4) * 32 + y * 4 + quarter
    in_lane = iota((128, LK), 0) == lane
    high = jnp.where(in_lane, (table_row >> 8) + 1, 0).astype(F32).astype(BF16)
    low = jnp.where(in_lane, table_row & 255, 0).astype(F32).astype(BF16)
    in_line = one_hot(iota((NY * NZ * 2, LK), 0) == line)
    codes = dot_t(in_line, high) * 256.0 + dot_t(in_line, low)
    rows_y_send[...] = codes.reshape(NY, 2 * NZ, 128)
    rows_y_recv[y] = rows_y_send[y]
    start(1, NY, along_y, y, rows_y_send, rows_y_recv)

    wait(recv_sems.at[0], NC, bags_recv)
    bags = bags_recv[...].reshape(128, 128).astype(F32)
    rolled = pltpu.roll(bags, 64, 1)
    left = iota((128, 128), 1) < 64
    spread = jnp.concatenate(
        [
            jnp.where(left, bags, 0.0),
            jnp.where(left, rolled, 0.0),
            jnp.where(left, 0.0, rolled),
            jnp.where(left, 0.0, bags),
        ],
        axis=0,
    ).astype(BF16)
    hot_parts = dot(count_parts, spread)
    hot_z_send[...] = (hot_parts[: NZ * 8] + hot_parts[NZ * 8 :]).reshape(NZ, 8, 128)
    hot_z_recv[z] = hot_z_send[z]
    start(3, NZ, along_z, z, hot_z_send, hot_z_recv)

    wait(recv_sems.at[1], NY, rows_y_recv)
    merged = jnp.sum(rows_y_recv[...], axis=0)
    for other in range(NZ):
        rows_z_send[other, 0:2] = merged[2 * other : 2 * other + 2]
        rows_z_send[other, 2:8] = jnp.zeros((6, 128), F32)
    rows_z_recv[z] = rows_z_send[z]
    start(4, NZ, along_z, z, rows_z_send, rows_z_recv)

    spot = one_hot(iota((NY * CAP, LK), 0) == half * (NY * 4) + owner_y * 4 + quarter)
    cold_place = place_of_bag(bag_ref[...].reshape(1, LK)) + 1
    weight = jnp.where(iota((16, LK), 0) == owner_z, cold_place, 0).astype(F32).astype(BF16)
    slot_place = dot_t(spot, weight).astype(jnp.int32)
    bag_number = iota((NY * CAP, 256), 1) + 1
    picks = []
    for other in range(NZ):
        pick = jnp.where(slot_place[:, other : other + 1] == bag_number, 1.0, 0.0)
        picks.append(jnp.concatenate([pick[: NY * 4], pick[NY * 4 :]], axis=1))
    pick = jnp.concatenate(picks, axis=0).astype(BF16)
    cold_send[...] = dot(pick, spread).reshape(NY * NZ, 4, 128).astype(BF16)
    cold_recv[row] = cold_send[row]

    def send_cold(other, device):
        pltpu.make_async_remote_copy(
            src_ref=cold_send.at[other],
            dst_ref=cold_recv.at[row],
            send_sem=send_sems.at[2],
            recv_sem=recv_sems.at[2],
            device_id=device,
            device_id_type=MESH,
        ).start()

    all_of_row(send_cold)

    wait(recv_sems.at[3], NZ, hot_z_recv)
    hot_y_recv[y] = jnp.sum(hot_z_recv[...], axis=0)
    start(6, NY, along_y, y, hot_y_recv, hot_y_recv)

    wait(recv_sems.at[4], NZ, rows_z_recv)
    code = jnp.concatenate(
        [jnp.sum(rows_z_recv[4 * g : 4 * g + 4], axis=0) for g in range(NZ // 4)], axis=1
    ).astype(jnp.int32)
    code_high, code_low = code >> 8, code & 255
    low_number = iota((256, LK), 0)
    land = [one_hot(code_low[side : side + 1] == low_number) for side in range(2)]

    wait(recv_sems.at[6], NY, hot_y_recv)
    hot_mine = jnp.sum(hot_y_recv[...], axis=0)
    hot_square_recv[col] = hot_mine * hot_mine
    start(9, NC, along_col, col, hot_square_recv, hot_square_recv)
    hot_all_recv[z] = hot_mine
    start(7, NZ, along_z, z, hot_all_recv, hot_all_recv)

    wait(recv_sems.at[2], NY * NZ, cold_recv)
    arrived = cold_recv[...].astype(F32).reshape(LK, 128).T
    grads = jnp.zeros((512, 256), F32)
    for side in range(2):
        mine = arrived[64 * side : 64 * side + 64]
        masked = jnp.concatenate(
            [jnp.where(code_high[side : side + 1] == h + 1, mine, 0.0) for h in range(8)], axis=0
        ).astype(BF16)
        grads += dot_t(masked, land[side])
    squares = []
    for h in range(8):
        part = grads[64 * h : 64 * h + 64]
        grad_ref[:, 256 * h : 256 * h + 256] = part
        squares.append(jnp.sum(part * part, axis=0, keepdims=True))
    square_recv[col] = jnp.concatenate(squares, axis=0)
    start(8, NC, along_col, col, square_recv, square_recv)

    def summed(ref):
        total = ref[0]
        for other in range(1, NC):
            total += ref[other]
        return total

    wait(recv_sems.at[9], NC, hot_square_recv)
    total = summed(hot_square_recv)
    sub, at_lane = iota((8, 128), 0), iota((8, 128), 1)
    first = jnp.sum(jnp.where(at_lane < 64, total, 0.0), axis=1, keepdims=True)
    second = jnp.sum(jnp.where(at_lane < 64, 0.0, total), axis=1, keepdims=True)
    both = jnp.where(((at_lane >> 3) & 1) == 0, first, second)
    here = ((at_lane & 7) == sub) & ((at_lane >> 4) == lax.rem(z, 8))
    hot_total_recv[z] = jnp.sum(jnp.where(here, both, 0.0), axis=0, keepdims=True)
    start(5, NZ, along_z, z, hot_total_recv, hot_total_recv)

    for fetch in fetches[6:]:
        fetch.wait()

    stores = []

    def store(source, target):
        copy = pltpu.make_async_copy(source, target, store_sems.at[len(stores)])
        copy.start()
        stores.append(copy)

    wait(recv_sems.at[8], NC, square_recv)
    total = summed(square_recv)
    for h in range(8):
        at = slice(256 * h, 256 * h + 256)
        accum = accum_ref[at].reshape(1, 256) + total[h : h + 1] / E
        new_accum_ref[at] = accum.reshape(256)
        scale = LR / (jnp.sqrt(accum) + EPS)
        new_ref[:, at] = table_ref[:, at] - grad_ref[:, at] * scale
        if h % 2 == 1:
            done = slice(256 * h - 256, 256 * h + 256)
            store(new_ref.at[:, done], new_hbm.at[:, done])
    store(new_accum_ref, new_accum_hbm)

    wait(recv_sems.at[7], NZ, hot_all_recv)
    pieces = []
    for other in range(NZ):
        piece = hot_all_recv[other]
        pieces += [piece, pltpu.roll(piece, 64, 1)]
    hot_grad = jnp.concatenate(pieces + [jnp.zeros((64, 128), F32)], axis=0).T[0:64]
    wait(recv_sems.at[5], NZ, hot_total_recv)
    hot_total = jnp.concatenate(
        [jnp.sum(hot_total_recv[0:8], axis=0), jnp.sum(hot_total_recv[8:12], axis=0)[:, 0:64]],
        axis=1,
    )
    accum = hot_accum_ref[...].reshape(1, 192) + hot_total / E
    new_hot_accum_ref[...] = accum.reshape(192)
    store(new_hot_accum_ref, new_hot_accum_hbm)
    new_hot_ref[...] = hot_table_ref[...] - hot_grad[:, 0:192] * (LR / (jnp.sqrt(accum) + EPS))
    store(new_hot_ref, new_hot_hbm)

    for stage, count, send in (
        (0, NC, bags_send),
        (1, NY, rows_y_send),
        (2, NY * NZ, cold_send),
        (3, NZ, hot_z_send),
        (4, NZ, rows_z_send),
        (5, NZ, hot_total_recv),
        (6, NY, hot_y_recv),
        (7, NZ, hot_all_recv),
        (8, NC, square_recv),
        (9, NC, hot_square_recv),
    ):
        wait(send_sems.at[stage], count, send)
    for copy in stores:
        copy.wait()


def exchange(*operands):
    hbm = pl.BlockSpec(memory_space=pltpu.HBM)
    return pl.pallas_call(
        exchange_kernel,
        out_shape=tuple(jax.ShapeDtypeStruct(a.shape, F32) for a in operands[6:]),
        in_specs=[hbm] * 10,
        out_specs=(hbm,) * 4,
        scratch_shapes=[
            *(pltpu.VMEM(a.shape, a.dtype) for a in operands),
            *(pltpu.VMEM(a.shape, F32) for a in operands[6:]),
            pltpu.VMEM((64, 2048), F32),
            pltpu.VMEM((NC, 16, 128), BF16),
            pltpu.VMEM((NC, 16, 128), BF16),
            pltpu.VMEM((NY, 2 * NZ, 128), F32),
            pltpu.VMEM((NY, 2 * NZ, 128), F32),
            pltpu.VMEM((NZ, 8, 128), F32),
            pltpu.VMEM((NZ, 8, 128), F32),
            pltpu.VMEM((NY * NZ, 4, 128), BF16),
            pltpu.VMEM((NY * NZ, 4, 128), BF16),
            pltpu.VMEM((NZ, 8, 128), F32),
            pltpu.VMEM((NZ, 8, 128), F32),
            pltpu.VMEM((NY, 8, 128), F32),
            pltpu.VMEM((NZ, 8, 128), F32),
            pltpu.VMEM((NC, 8, 256), F32),
            pltpu.VMEM((NC, 8, 128), F32),
            pltpu.VMEM((NZ, 1, 128), F32),
            pltpu.SemaphoreType.DMA((10,)),
            pltpu.SemaphoreType.DMA((7,)),
            pltpu.SemaphoreType.DMA((10,)),
            pltpu.SemaphoreType.DMA((10,)),
        ],
        compiler_params=pltpu.CompilerParams(
            collective_id=0, has_side_effects=True, vmem_limit_bytes=60 * 1024 * 1024
        ),
        name="exchange",
    )(*operands)


def write_kernel(*refs):
    sources, targets, holds, sems = refs[0:4], refs[4:8], refs[8:12], refs[12]
    rows = sources[0].shape[0] // 4
    parts = [(0, pl.ds(rows * part, rows)) for part in range(4)]
    parts += [(i, slice(None)) for i in range(1, 4)]
    loads, stores = [], []
    for n, (i, at) in enumerate(parts):
        loads.append(pltpu.make_async_copy(sources[i].at[at], holds[i].at[at], sems.at[0, n]))
        stores.append(pltpu.make_async_copy(holds[i].at[at], targets[i].at[at], sems.at[1, n]))
    for load in loads:
        load.start()
    for load, store in zip(loads, stores):
        load.wait()
        store.start()
    for store in stores:
        store.wait()


def write(*arrays):
    hbm = pl.BlockSpec(memory_space=pltpu.HBM)
    return pl.pallas_call(
        write_kernel,
        out_shape=tuple(jax.ShapeDtypeStruct(a.shape, a.dtype) for a in arrays),
        in_specs=[hbm] * 4,
        out_specs=(hbm,) * 4,
        scratch_shapes=[
            *(pltpu.VMEM(a.shape, a.dtype) for a in arrays),
            pltpu.SemaphoreType.DMA((2, 7)),
        ],
        compiler_params=pltpu.CompilerParams(vmem_limit_bytes=60 * 1024 * 1024),
        name="write",
    )(*arrays)


def on_device(
    pooled_grad,
    cold_table,
    cold_accum,
    hot_table,
    hot_accum,
    cold_owner,
    cold_row,
    cold_bag,
    hot_id,
    hot_bag,
):
    updated = exchange(
        pooled_grad.reshape(32, E),
        cold_owner.T,
        cold_row,
        cold_bag,
        hot_id,
        hot_bag,
        cold_table,
        cold_accum,
        hot_table,
        hot_accum,
    )
    return tuple(write(*updated))


def solution(mesh):
    in_specs = (
        P(("row", "col"), None, None),
        P("col", "row"),
        P("row"),
        P("col", None),
        P(),
        P("row", None),
        P("row"),
        P("row"),
        P("row"),
        P("row"),
    )
    out_specs = (P("col", "row"), P("row"), P("col", None), P())
    return jax.shard_map(
        on_device, mesh=mesh, in_specs=in_specs, out_specs=out_specs, check_vma=False
    )
```

```python
import jax
import jax.numpy as jnp
from jax import lax
from jax.experimental import pallas as pl
from jax.experimental.pallas import tpu as pltpu
from jax.sharding import PartitionSpec as P

E = 512
LR = 0.3
EPS = 1e-08
MESH = pl.DeviceIdType.MESH

NC = 8
NY = 8
NZ = 12
LK = 384
LH = 512
CAP = 8
F32 = jnp.float32
BF16 = jnp.bfloat16


def iota(shape, dim):
    return lax.broadcasted_iota(jnp.int32, shape, dim)


def one_hot(mask):
    return jnp.where(mask, 1.0, 0.0).astype(BF16)


def dot(a, b):
    return jnp.dot(a, b, preferred_element_type=F32)


def dot_t(a, b):
    return lax.dot_general(a, b, (((1,), (1,)), ((), ())), preferred_element_type=F32)


def exchange_kernel(
    pool_hbm,
    owner_hbm,
    row_hbm,
    bag_hbm,
    hot_id_hbm,
    hot_bag_hbm,
    table_hbm,
    accum_hbm,
    hot_table_hbm,
    hot_accum_hbm,
    new_hbm,
    new_accum_hbm,
    new_hot_hbm,
    new_hot_accum_hbm,
    pool_ref,
    owner_ref,
    row_ref,
    bag_ref,
    hot_id_ref,
    hot_bag_ref,
    table_ref,
    accum_ref,
    hot_table_ref,
    hot_accum_ref,
    new_ref,
    new_accum_ref,
    new_hot_ref,
    new_hot_accum_ref,
    grad_ref,
    bags_send,
    bags_recv,
    rows_y_send,
    rows_y_recv,
    rows_z_send,
    rows_z_recv,
    cold_send,
    cold_recv,
    hot_z_send,
    hot_z_recv,
    hot_y_recv,
    hot_all_recv,
    square_recv,
    hot_square_recv,
    hot_total_recv,
    fetch_sems,
    store_sems,
    send_sems,
    recv_sems,
    relay_sems,
):
    row = lax.axis_index("row")
    col = lax.axis_index("col")
    z = lax.div(row, NY)
    y = lax.rem(row, NY)

    def along_col(k):
        other = lax.rem(col + k, NC)
        return other, {"row": row, "col": other}

    def along_y(k):
        other = lax.rem(y + k, NY)
        return other, {"row": z * NY + other, "col": col}

    def along_z(k):
        other = lax.rem(z + k, NZ)
        return other, {"row": other * NY + y, "col": col}

    def start(stage, count, along, me, send, recv):
        for k in sorted(range(1, count), key=lambda k: -min(k, count - k)):
            other, device = along(k)
            pltpu.make_async_remote_copy(
                src_ref=send.at[me if send is recv else other],
                dst_ref=recv.at[me],
                send_sem=send_sems.at[stage],
                recv_sem=recv_sems.at[stage],
                device_id=device,
                device_id_type=MESH,
            ).start()

    def wait(sem, count, ref):
        part = ref.at[pl.ds(0, count - 1)]
        pltpu.make_async_copy(part, part, sem).wait()

    fetches = [
        pltpu.make_async_copy(source, target, fetch_sems.at[i])
        for i, (source, target) in enumerate(
            (
                (pool_hbm, pool_ref),
                (owner_hbm, owner_ref),
                (row_hbm, row_ref),
                (bag_hbm, bag_ref),
                (hot_id_hbm, hot_id_ref),
                (hot_bag_hbm, hot_bag_ref),
                (table_hbm, table_ref),
                (accum_hbm, accum_ref),
                (hot_table_hbm, hot_table_ref),
                (hot_accum_hbm, hot_accum_ref),
            )
        )
    ]
    for fetch in fetches:
        fetch.start()
    barrier = pltpu.get_barrier_semaphore()
    near_z, near_y = NZ // 4, NY // 4
    greeted = [along_col(k)[1] for k in range(1, NC)]
    greeted += [along_z(k)[1] for k in range(1, near_z + 1)]
    greeted += [along_z(NZ - k)[1] for k in range(1, near_z + 1)]
    greeted += [along_y(k)[1] for k in range(1, near_y + 1)]
    greeted += [along_y(NY - k)[1] for k in range(1, near_y + 1)]
    for device in greeted:
        pl.semaphore_signal(barrier, inc=1, device_id=device, device_id_type=MESH)

    def around(step_z, step_y):
        other = lax.rem(z + step_z, NZ) * NY + lax.rem(y + step_y, NY)
        return other, {"row": other, "col": col}

    def rings(first, last, act):
        def ring(i, carry):
            step_z = NZ // 2 + (1 - 2 * lax.rem(i, 2)) * lax.div(i + 1, 2)
            for step_y in (4, 3, 5, 2, 6, 1, 7, 0):
                act(*around(step_z, step_y))
            return carry

        lax.fori_loop(first, last, ring, 0)

    fetches[0].wait()

    low_lanes = iota((16, 128), 1) < 64
    for pair in range(NC // 2):
        first = pool_ref[0:16, pair * 128 : pair * 128 + 128].astype(F32)
        second = pool_ref[16:32, pair * 128 : pair * 128 + 128].astype(F32)
        bags_send[2 * pair] = jnp.where(low_lanes, first, pltpu.roll(second, 64, 1)).astype(BF16)
        bags_send[2 * pair + 1] = jnp.where(low_lanes, pltpu.roll(first, 64, 1), second).astype(BF16)
    bags_recv[col] = bags_send[col]
    pl.semaphore_wait(barrier, len(greeted))
    start(0, NC, along_col, col, bags_send, bags_recv)
    for i, (along, count, step) in enumerate(((along_z, NZ, near_z), (along_y, NY, near_y))):
        for k in (step, count - step):
            pl.semaphore_signal(
                relay_sems.at[i], inc=1, device_id=along(k)[1], device_id_type=MESH
            )

    def place_of_bag(bag):
        return ((bag >> 4) & 1) * 128 + (bag >> 5) * 16 + (bag & 15)

    for fetch in fetches[1:6]:
        fetch.wait()
    hot_id = hot_id_ref[...].reshape(1, LH)
    hot_line = (hot_id >> 4) * 8 + (hot_id & 7) + ((hot_id >> 3) & 1) * (NZ * 8)
    hot_rows = one_hot(iota((NZ * 16, LH), 0) == hot_line)
    hot_place = place_of_bag(hot_bag_ref[...].reshape(1, LH))
    counts = dot_t(hot_rows, one_hot(iota((256, LH), 0) == hot_place))
    counts = jnp.concatenate([counts[: NZ * 8], counts[NZ * 8 :]], axis=1)
    count_high = counts.astype(BF16)
    count_low = (counts - count_high.astype(F32)).astype(BF16)
    count_parts = jnp.concatenate([count_high, count_low], axis=0)

    owner = owner_ref[...].reshape(1, LK)
    target = iota((NY * NZ, LK), 0) == owner
    taken = one_hot(target)
    earlier = one_hot(iota((128, 128), 0) < iota((128, 128), 1))
    carry = jnp.zeros((NY * NZ, 1), F32)
    ranks = []
    for part in range(LK // 128):
        at = slice(128 * part, 128 * part + 128)
        before = dot(taken[:, at], earlier) + carry
        ranks.append(jnp.sum(jnp.where(target[:, at], before, 0.0), axis=0, keepdims=True))
        carry += jnp.sum(jnp.where(target[:, at], 1.0, 0.0), axis=1, keepdims=True)
    rank = jnp.concatenate(ranks, axis=1).astype(jnp.int32)
    owner_z, owner_y = owner >> 3, owner & 7
    half, quarter = rank >> 2, rank & 3
    table_row = row_ref[...].reshape(1, LK)
    line = owner_y * (2 * NZ) + owner_z * 2 + half
    lane = lax.rem(z, 4) * 32 + y * 4 + quarter
    in_lane = iota((128, LK), 0) == lane
    high = jnp.where(in_lane, (table_row >> 8) + 1, 0).astype(F32).astype(BF16)
    low = jnp.where(in_lane, table_row & 255, 0).astype(F32).astype(BF16)
    in_line = one_hot(iota((NY * NZ * 2, LK), 0) == line)
    codes = dot_t(in_line, high) * 256.0 + dot_t(in_line, low)
    rows_y_send[...] = codes.reshape(NY, 2 * NZ, 128)
    rows_y_recv[y] = rows_y_send[y]
    pl.semaphore_wait(relay_sems.at[0], 2)
    pl.semaphore_wait(relay_sems.at[1], 2)
    start(1, NY, along_y, y, rows_y_send, rows_y_recv)

    wait(recv_sems.at[0], NC, bags_recv)
    bags = bags_recv[...].reshape(128, 128).astype(F32)
    rolled = pltpu.roll(bags, 64, 1)
    left = iota((128, 128), 1) < 64
    spread = jnp.concatenate(
        [
            jnp.where(left, bags, 0.0),
            jnp.where(left, rolled, 0.0),
            jnp.where(left, 0.0, rolled),
            jnp.where(left, 0.0, bags),
        ],
        axis=0,
    ).astype(BF16)
    hot_parts = dot(count_parts, spread)
    hot_z_send[...] = (hot_parts[: NZ * 8] + hot_parts[NZ * 8 :]).reshape(NZ, 8, 128)
    hot_z_recv[z] = hot_z_send[z]
    start(3, NZ, along_z, z, hot_z_send, hot_z_recv)

    wait(recv_sems.at[1], NY, rows_y_recv)
    merged = jnp.sum(rows_y_recv[...], axis=0)
    for other in range(NZ):
        rows_z_send[other, 0:2] = merged[2 * other : 2 * other + 2]
        rows_z_send[other, 2:8] = jnp.zeros((6, 128), F32)
    rows_z_recv[z] = rows_z_send[z]
    start(4, NZ, along_z, z, rows_z_send, rows_z_recv)

    spot = one_hot(iota((NY * CAP, LK), 0) == half * (NY * 4) + owner_y * 4 + quarter)
    cold_place = place_of_bag(bag_ref[...].reshape(1, LK)) + 1
    weight = jnp.where(iota((16, LK), 0) == owner_z, cold_place, 0).astype(F32).astype(BF16)
    slot_place = dot_t(spot, weight).astype(jnp.int32)
    bag_number = iota((NY * CAP, 256), 1) + 1
    picks = []
    for other in range(NZ):
        pick = jnp.where(slot_place[:, other : other + 1] == bag_number, 1.0, 0.0)
        picks.append(jnp.concatenate([pick[: NY * 4], pick[NY * 4 :]], axis=1))
    pick = jnp.concatenate(picks, axis=0).astype(BF16)
    cold_send[...] = dot(pick, spread).reshape(NY * NZ, 4, 128).astype(BF16)
    cold_recv[row] = cold_send[row]

    def send_cold(other, device):
        pltpu.make_async_remote_copy(
            src_ref=cold_send.at[other],
            dst_ref=cold_recv.at[row],
            send_sem=send_sems.at[2],
            recv_sem=recv_sems.at[2],
            device_id=device,
            device_id_type=MESH,
        ).start()

    rings(0, 7, send_cold)

    wait(recv_sems.at[3], NZ, hot_z_recv)
    hot_y_recv[y] = jnp.sum(hot_z_recv[...], axis=0)
    start(6, NY, along_y, y, hot_y_recv, hot_y_recv)

    rings(7, NZ - 1, send_cold)
    for step_y in (4, 3, 5, 2, 6, 1, 7):
        send_cold(*around(0, step_y))

    wait(recv_sems.at[4], NZ, rows_z_recv)
    code = jnp.concatenate(
        [jnp.sum(rows_z_recv[4 * g : 4 * g + 4], axis=0) for g in range(NZ // 4)], axis=1
    ).astype(jnp.int32)
    code_high, code_low = code >> 8, code & 255
    low_number = iota((256, LK), 0)
    land = [one_hot(code_low[side : side + 1] == low_number) for side in range(2)]

    wait(recv_sems.at[6], NY, hot_y_recv)
    hot_mine = jnp.sum(hot_y_recv[...], axis=0)
    hot_square_recv[col] = hot_mine * hot_mine
    start(9, NC, along_col, col, hot_square_recv, hot_square_recv)
    hot_all_recv[z] = hot_mine
    start(7, NZ, along_z, z, hot_all_recv, hot_all_recv)

    wait(recv_sems.at[2], NY * NZ, cold_recv)
    arrived = cold_recv[...].astype(F32).reshape(LK, 128).T
    grads = jnp.zeros((512, 256), F32)
    for side in range(2):
        mine = arrived[64 * side : 64 * side + 64]
        masked = jnp.concatenate(
            [jnp.where(code_high[side : side + 1] == h + 1, mine, 0.0) for h in range(8)], axis=0
        ).astype(BF16)
        grads += dot_t(masked, land[side])
    squares = []
    for h in range(8):
        part = grads[64 * h : 64 * h + 64]
        grad_ref[:, 256 * h : 256 * h + 256] = part
        squares.append(jnp.sum(part * part, axis=0, keepdims=True))
    square_recv[col] = jnp.concatenate(squares, axis=0)
    start(8, NC, along_col, col, square_recv, square_recv)

    def summed(ref):
        total = ref[0]
        for other in range(1, NC):
            total += ref[other]
        return total

    wait(recv_sems.at[9], NC, hot_square_recv)
    total = summed(hot_square_recv)
    sub, at_lane = iota((8, 128), 0), iota((8, 128), 1)
    first = jnp.sum(jnp.where(at_lane < 64, total, 0.0), axis=1, keepdims=True)
    second = jnp.sum(jnp.where(at_lane < 64, 0.0, total), axis=1, keepdims=True)
    both = jnp.where(((at_lane >> 3) & 1) == 0, first, second)
    here = ((at_lane & 7) == sub) & ((at_lane >> 4) == lax.rem(z, 8))
    hot_total_recv[z] = jnp.sum(jnp.where(here, both, 0.0), axis=0, keepdims=True)
    start(5, NZ, along_z, z, hot_total_recv, hot_total_recv)

    for fetch in fetches[6:]:
        fetch.wait()

    stores = []

    def store(source, target):
        copy = pltpu.make_async_copy(source, target, store_sems.at[len(stores)])
        copy.start()
        stores.append(copy)

    wait(recv_sems.at[8], NC, square_recv)
    total = summed(square_recv)
    for h in range(8):
        at = slice(256 * h, 256 * h + 256)
        accum = accum_ref[at].reshape(1, 256) + total[h : h + 1] / E
        new_accum_ref[at] = accum.reshape(256)
        scale = LR / (jnp.sqrt(accum) + EPS)
        new_ref[:, at] = table_ref[:, at] - grad_ref[:, at] * scale
        if h % 2 == 1:
            done = slice(256 * h - 256, 256 * h + 256)
            store(new_ref.at[:, done], new_hbm.at[:, done])
    store(new_accum_ref, new_accum_hbm)

    wait(recv_sems.at[7], NZ, hot_all_recv)
    pieces = []
    for other in range(NZ):
        piece = hot_all_recv[other]
        pieces += [piece, pltpu.roll(piece, 64, 1)]
    hot_grad = jnp.concatenate(pieces + [jnp.zeros((64, 128), F32)], axis=0).T[0:64]
    wait(recv_sems.at[5], NZ, hot_total_recv)
    hot_total = jnp.concatenate(
        [jnp.sum(hot_total_recv[0:8], axis=0), jnp.sum(hot_total_recv[8:12], axis=0)[:, 0:64]],
        axis=1,
    )
    accum = hot_accum_ref[...].reshape(1, 192) + hot_total / E
    new_hot_accum_ref[...] = accum.reshape(192)
    store(new_hot_accum_ref, new_hot_accum_hbm)
    new_hot_ref[...] = hot_table_ref[...] - hot_grad[:, 0:192] * (LR / (jnp.sqrt(accum) + EPS))
    store(new_hot_ref, new_hot_hbm)

    for stage, count, send in (
        (0, NC, bags_send),
        (1, NY, rows_y_send),
        (2, NY * NZ, cold_send),
        (3, NZ, hot_z_send),
        (4, NZ, rows_z_send),
        (5, NZ, hot_total_recv),
        (6, NY, hot_y_recv),
        (7, NZ, hot_all_recv),
        (8, NC, square_recv),
        (9, NC, hot_square_recv),
    ):
        wait(send_sems.at[stage], count, send)
    for copy in stores:
        copy.wait()


def exchange(*operands):
    hbm = pl.BlockSpec(memory_space=pltpu.HBM)
    return pl.pallas_call(
        exchange_kernel,
        out_shape=tuple(jax.ShapeDtypeStruct(a.shape, F32) for a in operands[6:]),
        in_specs=[hbm] * 10,
        out_specs=(hbm,) * 4,
        scratch_shapes=[
            *(pltpu.VMEM(a.shape, a.dtype) for a in operands),
            *(pltpu.VMEM(a.shape, F32) for a in operands[6:]),
            pltpu.VMEM((64, 2048), F32),
            pltpu.VMEM((NC, 16, 128), BF16),
            pltpu.VMEM((NC, 16, 128), BF16),
            pltpu.VMEM((NY, 2 * NZ, 128), F32),
            pltpu.VMEM((NY, 2 * NZ, 128), F32),
            pltpu.VMEM((NZ, 8, 128), F32),
            pltpu.VMEM((NZ, 8, 128), F32),
            pltpu.VMEM((NY * NZ, 4, 128), BF16),
            pltpu.VMEM((NY * NZ, 4, 128), BF16),
            pltpu.VMEM((NZ, 8, 128), F32),
            pltpu.VMEM((NZ, 8, 128), F32),
            pltpu.VMEM((NY, 8, 128), F32),
            pltpu.VMEM((NZ, 8, 128), F32),
            pltpu.VMEM((NC, 8, 256), F32),
            pltpu.VMEM((NC, 8, 128), F32),
            pltpu.VMEM((NZ, 1, 128), F32),
            pltpu.SemaphoreType.DMA((10,)),
            pltpu.SemaphoreType.DMA((7,)),
            pltpu.SemaphoreType.DMA((10,)),
            pltpu.SemaphoreType.DMA((10,)),
            pltpu.SemaphoreType.REGULAR((2,)),
        ],
        compiler_params=pltpu.CompilerParams(
            collective_id=0, has_side_effects=True, vmem_limit_bytes=60 * 1024 * 1024
        ),
        name="exchange",
    )(*operands)


def write_kernel(*refs):
    sources, targets, holds, sems = refs[0:4], refs[4:8], refs[8:12], refs[12]
    rows = sources[0].shape[0] // 4
    parts = [(0, pl.ds(rows * part, rows)) for part in range(4)]
    parts += [(i, slice(None)) for i in range(1, 4)]
    loads, stores = [], []
    for n, (i, at) in enumerate(parts):
        loads.append(pltpu.make_async_copy(sources[i].at[at], holds[i].at[at], sems.at[0, n]))
        stores.append(pltpu.make_async_copy(holds[i].at[at], targets[i].at[at], sems.at[1, n]))
    for load in loads:
        load.start()
    for load, store in zip(loads, stores):
        load.wait()
        store.start()
    for store in stores:
        store.wait()


def write(*arrays):
    hbm = pl.BlockSpec(memory_space=pltpu.HBM)
    return pl.pallas_call(
        write_kernel,
        out_shape=tuple(jax.ShapeDtypeStruct(a.shape, a.dtype) for a in arrays),
        in_specs=[hbm] * 4,
        out_specs=(hbm,) * 4,
        scratch_shapes=[
            *(pltpu.VMEM(a.shape, a.dtype) for a in arrays),
            pltpu.SemaphoreType.DMA((2, 7)),
        ],
        compiler_params=pltpu.CompilerParams(vmem_limit_bytes=60 * 1024 * 1024),
        name="write",
    )(*arrays)


def on_device(
    pooled_grad,
    cold_table,
    cold_accum,
    hot_table,
    hot_accum,
    cold_owner,
    cold_row,
    cold_bag,
    hot_id,
    hot_bag,
):
    updated = exchange(
        pooled_grad.reshape(32, E),
        cold_owner.T,
        cold_row,
        cold_bag,
        hot_id,
        hot_bag,
        cold_table,
        cold_accum,
        hot_table,
        hot_accum,
    )
    return tuple(write(*updated))


def solution(mesh):
    in_specs = (
        P(("row", "col"), None, None),
        P("col", "row"),
        P("row"),
        P("col", None),
        P(),
        P("row", None),
        P("row"),
        P("row"),
        P("row"),
        P("row"),
    )
    out_specs = (P("col", "row"), P("row"), P("col", None), P())
    return jax.shard_map(
        on_device, mesh=mesh, in_specs=in_specs, out_specs=out_specs, check_vma=False
    )
```

```python
import jax
import jax.numpy as jnp
from jax import lax
from jax.experimental import pallas as pl
from jax.experimental.pallas import tpu as pltpu
from jax.sharding import PartitionSpec as P

E = 512
LR = 0.3
EPS = 1e-08
MESH = pl.DeviceIdType.MESH

NC = 8
NY = 8
NX = 4
NZ = 12
LK = 384
LH = 512
CAP = 8
F32 = jnp.float32
BF16 = jnp.bfloat16


def iota(shape, dim):
    return lax.broadcasted_iota(jnp.int32, shape, dim)


def one_hot(mask):
    return jnp.where(mask, 1.0, 0.0).astype(BF16)


def dot(a, b):
    return jnp.dot(a, b, preferred_element_type=F32)


def dot_t(a, b):
    return lax.dot_general(a, b, (((1,), (1,)), ((), ())), preferred_element_type=F32)


def exchange_kernel(
    pool_hbm,
    owner_hbm,
    row_hbm,
    bag_hbm,
    hot_id_hbm,
    hot_bag_hbm,
    table_hbm,
    accum_hbm,
    hot_table_hbm,
    hot_accum_hbm,
    new_hbm,
    new_accum_hbm,
    new_hot_hbm,
    new_hot_accum_hbm,
    pool_ref,
    owner_ref,
    row_ref,
    bag_ref,
    hot_id_ref,
    hot_bag_ref,
    table_ref,
    accum_ref,
    hot_table_ref,
    hot_accum_ref,
    new_ref,
    new_accum_ref,
    new_hot_ref,
    new_hot_accum_ref,
    grad_ref,
    land_ref,
    bags_send,
    bags_recv,
    rows_y_send,
    rows_y_recv,
    rows_z_send,
    rows_z_recv,
    cold_send,
    cold_recv,
    hot_z_send,
    hot_z_recv,
    hot_y_recv,
    hot_all_recv,
    square_recv,
    hot_square_recv,
    hot_total_recv,
    fetch_sems,
    store_sems,
    send_sems,
    recv_sems,
    relay_sems,
):
    row = lax.axis_index("row")
    col = lax.axis_index("col")
    z = lax.div(row, NY)
    y = lax.rem(row, NY)

    def along_col(k):
        other = lax.rem(col + k, NC)
        return other, {"row": row, "col": other}

    def along_y(k):
        other = lax.rem(y + k, NY)
        return other, {"row": z * NY + other, "col": col}

    def along_z(k):
        other = lax.rem(z + k, NZ)
        return other, {"row": other * NY + y, "col": col}

    def along_core(k):
        other = col + k - 2 * lax.rem(col, 2)
        return other, {"row": row, "col": other}

    def start(stage, count, along, me, send, recv):
        for k in sorted(range(1, count), key=lambda k: -min(k, count - k)):
            other, device = along(k)
            pltpu.make_async_remote_copy(
                src_ref=send.at[me if send is recv else other],
                dst_ref=recv.at[me],
                send_sem=send_sems.at[stage],
                recv_sem=recv_sems.at[stage],
                device_id=device,
                device_id_type=MESH,
            ).start()

    def wait(sem, count, ref):
        part = ref.at[pl.ds(0, count - 1)]
        pltpu.make_async_copy(part, part, sem).wait()

    fetches = [
        pltpu.make_async_copy(source, target, fetch_sems.at[i])
        for i, (source, target) in enumerate(
            (
                (pool_hbm, pool_ref),
                (owner_hbm, owner_ref),
                (row_hbm, row_ref),
                (bag_hbm, bag_ref),
                (hot_id_hbm, hot_id_ref),
                (hot_bag_hbm, hot_bag_ref),
                (table_hbm, table_ref),
                (accum_hbm, accum_ref),
                (hot_table_hbm, hot_table_ref),
                (hot_accum_hbm, hot_accum_ref),
            )
        )
    ]
    fetches[0].start()
    barrier = pltpu.get_barrier_semaphore()
    near_z, near_y = NZ // 4, NY // 4
    greeted = []
    for along, count, near in ((along_z, NZ, near_z), (along_y, NY, near_y), (along_col, NC, NC // 2)):
        steps = {k for step in range(1, near + 1) for k in (step, count - step)}
        for k in sorted(steps, key=lambda k: -min(k, count - k)):
            greeted.append(along(k)[1])
    for device in greeted:
        pl.semaphore_signal(barrier, inc=1, device_id=device, device_id_type=MESH)
    for fetch in fetches[1:]:
        fetch.start()

    def around(step_z, step_y):
        other = lax.rem(z + step_z, NZ) * NY + lax.rem(y + step_y, NY)
        return other, {"row": other, "col": col}

    def rings(first, last, act):
        def ring(i, carry):
            step_z = NZ // 2 + (1 - 2 * lax.rem(i, 2)) * lax.div(i + 1, 2)
            for step_y in (4, 3, 5, 2, 6, 1, 7, 0):
                act(*around(step_z, step_y))
            return carry

        lax.fori_loop(first, last, ring, 0)

    fetches[0].wait()

    low_lanes = iota((16, 128), 1) < 64
    for pair in range(NC // 2):
        first = pool_ref[0:16, pair * 128 : pair * 128 + 128].astype(F32)
        second = pool_ref[16:32, pair * 128 : pair * 128 + 128].astype(F32)
        bags_send[2 * pair] = jnp.where(low_lanes, first, pltpu.roll(second, 64, 1)).astype(BF16)
        bags_send[2 * pair + 1] = jnp.where(low_lanes, pltpu.roll(first, 64, 1), second).astype(BF16)
    bags_recv[col] = bags_send[col]
    pl.semaphore_wait(barrier, len(greeted))
    start(0, NC, along_col, col, bags_send, bags_recv)
    for i, (along, count, step) in enumerate(((along_z, NZ, near_z), (along_y, NY, near_y))):
        for k in (step, count - step):
            pl.semaphore_signal(
                relay_sems.at[i], inc=1, device_id=along(k)[1], device_id_type=MESH
            )

    def place_of_bag(bag):
        return ((bag >> 4) & 1) * 128 + (bag >> 5) * 16 + (bag & 15)

    for fetch in fetches[1:6]:
        fetch.wait()
    hot_id = hot_id_ref[...].reshape(1, LH)
    hot_line = (hot_id >> 4) * 8 + (hot_id & 7) + ((hot_id >> 3) & 1) * (NZ * 8)
    hot_rows = one_hot(iota((NZ * 16, LH), 0) == hot_line)
    hot_place = place_of_bag(hot_bag_ref[...].reshape(1, LH))
    counts = dot_t(hot_rows, one_hot(iota((256, LH), 0) == hot_place))
    counts = jnp.concatenate([counts[: NZ * 8], counts[NZ * 8 :]], axis=1)
    count_high = counts.astype(BF16)
    count_low = (counts - count_high.astype(F32)).astype(BF16)
    count_parts = jnp.concatenate([count_high, count_low], axis=0)

    owner = owner_ref[...].reshape(1, LK)
    target = iota((NY * NZ, LK), 0) == owner
    taken = one_hot(target)
    earlier = one_hot(iota((128, 128), 0) < iota((128, 128), 1))
    carry = jnp.zeros((NY * NZ, 1), F32)
    ranks = []
    for part in range(LK // 128):
        at = slice(128 * part, 128 * part + 128)
        before = dot(taken[:, at], earlier) + carry
        ranks.append(jnp.sum(jnp.where(target[:, at], before, 0.0), axis=0, keepdims=True))
        carry += jnp.sum(jnp.where(target[:, at], 1.0, 0.0), axis=1, keepdims=True)
    rank = jnp.concatenate(ranks, axis=1).astype(jnp.int32)
    owner_z, owner_y = owner >> 3, owner & 7
    half, quarter = rank >> 2, rank & 3
    table_row = row_ref[...].reshape(1, LK)
    line = owner_y * (2 * NZ) + owner_z * 2 + half
    lane = lax.rem(z, 4) * 32 + y * 4 + quarter
    in_lane = iota((128, LK), 0) == lane
    high = jnp.where(in_lane, (table_row >> 8) + 1, 0).astype(F32).astype(BF16)
    low = jnp.where(in_lane, table_row & 255, 0).astype(F32).astype(BF16)
    in_line = one_hot(iota((NY * NZ * 2, LK), 0) == line)
    codes = dot_t(in_line, high) * 256.0 + dot_t(in_line, low)
    rows_y_send[...] = codes.reshape(NY, 2 * NZ, 128)
    rows_y_recv[y] = rows_y_send[y]
    pl.semaphore_wait(relay_sems.at[0], 2)
    pl.semaphore_wait(relay_sems.at[1], 2)
    start(1, NY, along_y, y, rows_y_send, rows_y_recv)

    wait(recv_sems.at[0], NC, bags_recv)
    bags = bags_recv[...].reshape(128, 128).astype(F32)
    rolled = pltpu.roll(bags, 64, 1)
    left = iota((128, 128), 1) < 64
    spread = jnp.concatenate(
        [
            jnp.where(left, bags, 0.0),
            jnp.where(left, rolled, 0.0),
            jnp.where(left, 0.0, rolled),
            jnp.where(left, 0.0, bags),
        ],
        axis=0,
    ).astype(BF16)
    hot_parts = dot(count_parts, spread)
    hot_z_send[...] = (hot_parts[: NZ * 8] + hot_parts[NZ * 8 :]).reshape(NZ, 8, 128)
    start(3, NZ, along_z, z, hot_z_send, hot_z_recv)
    hot_z_recv[z] = hot_z_send[z]

    wait(recv_sems.at[1], NY, rows_y_recv)
    merged = jnp.sum(rows_y_recv[...], axis=0)
    for other in range(NZ):
        rows_z_send[other, 0:2] = merged[2 * other : 2 * other + 2]
        rows_z_send[other, 2:8] = jnp.zeros((6, 128), F32)
    rows_z_recv[z] = rows_z_send[z]
    start(4, NZ, along_z, z, rows_z_send, rows_z_recv)

    spot = one_hot(iota((NY * CAP, LK), 0) == half * (NY * 4) + owner_y * 4 + quarter)
    cold_place = place_of_bag(bag_ref[...].reshape(1, LK)) + 1
    weight = jnp.where(iota((16, LK), 0) == owner_z, cold_place, 0).astype(F32).astype(BF16)
    slot_place = dot_t(spot, weight).astype(jnp.int32)
    bag_number = iota((NY * CAP, 256), 1) + 1
    picks = []
    for other in range(NZ):
        pick = jnp.where(slot_place[:, other : other + 1] == bag_number, 1.0, 0.0)
        picks.append(jnp.concatenate([pick[: NY * 4], pick[NY * 4 :]], axis=1))
    pick = jnp.concatenate(picks, axis=0).astype(BF16)
    cold_send[...] = dot(pick, spread).reshape(NY * NZ, 4, 128).astype(BF16)
    cold_recv[row] = cold_send[row]

    def send_cold(other, device):
        pltpu.make_async_remote_copy(
            src_ref=cold_send.at[other],
            dst_ref=cold_recv.at[row],
            send_sem=send_sems.at[2],
            recv_sem=recv_sems.at[2],
            device_id=device,
            device_id_type=MESH,
        ).start()

    rings(0, 7, send_cold)

    wait(recv_sems.at[3], NZ, hot_z_recv)
    hot_y_recv[y] = jnp.sum(hot_z_recv[...], axis=0)
    start(6, NY, along_y, y, hot_y_recv, hot_y_recv)

    rings(7, NZ - 1, send_cold)
    for step_y in (4, 3, 5, 2, 6, 1, 7):
        send_cold(*around(0, step_y))

    wait(recv_sems.at[4], NZ, rows_z_recv)
    code = jnp.concatenate(
        [jnp.sum(rows_z_recv[4 * g : 4 * g + 4], axis=0) for g in range(NZ // 4)], axis=1
    ).astype(jnp.int32)
    code_high, code_low = code >> 8, code & 255
    low_number = iota((256, LK), 0)
    land = jnp.concatenate(
        [jnp.where(code_low[side : side + 1] == low_number, 1.0, 0.0).T for side in range(2)], axis=0
    )
    land_ref[...] = land.astype(BF16)

    wait(recv_sems.at[6], NY, hot_y_recv)
    hot_mine = jnp.sum(hot_y_recv[...], axis=0)
    core, chip_x = lax.rem(col, 2), lax.div(col, 2)
    hot_square_recv[core] = hot_mine * hot_mine
    start(9, 2, along_core, core, hot_square_recv, hot_square_recv)
    hot_all_recv[z] = hot_mine
    start(7, NZ, along_z, z, hot_all_recv, hot_all_recv)

    wait(recv_sems.at[9], 2, hot_square_recv)
    total = hot_square_recv[0] + hot_square_recv[1]
    sub, at_lane = iota((8, 128), 0), iota((8, 128), 1)
    first = jnp.sum(jnp.where(at_lane < 64, total, 0.0), axis=1, keepdims=True)
    second = jnp.sum(jnp.where(at_lane < 64, 0.0, total), axis=1, keepdims=True)
    both = jnp.where(((at_lane >> 3) & 1) == 0, first, second)
    here = ((at_lane & 7) == sub) & ((at_lane >> 4) == lax.rem(z, 8))
    mine_at = z * NX + chip_x
    hot_total_recv[mine_at] = jnp.sum(jnp.where(here, both, 0.0), axis=0, keepdims=True)

    def send_total(step_z, step_x):
        device = {
            "row": lax.rem(z + step_z, NZ) * NY + y,
            "col": lax.rem(chip_x + step_x, NX) * 2 + core,
        }
        pltpu.make_async_remote_copy(
            src_ref=hot_total_recv.at[mine_at],
            dst_ref=hot_total_recv.at[mine_at],
            send_sem=send_sems.at[5],
            recv_sem=recv_sems.at[5],
            device_id=device,
            device_id_type=MESH,
        ).start()

    by_distance = sorted(
        ((step_z, step_x) for step_z in range(NZ) for step_x in range(NX)),
        key=lambda s: -(min(s[0], NZ - s[0]) + min(s[1], NX - s[1])),
    )[:-1]
    for steps in by_distance[:18]:
        send_total(*steps)

    wait(recv_sems.at[2], NY * NZ, cold_recv)
    arrived = cold_recv[...].astype(F32).reshape(LK, 128).T
    masked = []
    for side in range(2):
        mine = arrived[64 * side : 64 * side + 64]
        blocks = [jnp.where(code_high[side : side + 1] == h + 1, mine, 0.0) for h in range(8)]
        masked.append(jnp.concatenate(blocks, axis=0).astype(BF16))
    grads = dot(jnp.concatenate(masked, axis=1), land_ref[...])
    squares = []
    for h in range(8):
        part = grads[64 * h : 64 * h + 64]
        grad_ref[:, 256 * h : 256 * h + 256] = part
        squares.append(jnp.sum(part * part, axis=0, keepdims=True))
    square_recv[col] = jnp.concatenate(squares, axis=0)
    start(8, NC, along_col, col, square_recv, square_recv)

    def summed(ref):
        total = ref[0]
        for other in range(1, NC):
            total += ref[other]
        return total

    for steps in by_distance[18:]:
        send_total(*steps)
    for fetch in fetches[6:]:
        fetch.wait()

    stores = []

    def store(source, target):
        copy = pltpu.make_async_copy(source, target, store_sems.at[len(stores)])
        copy.start()
        stores.append(copy)

    wait(recv_sems.at[8], NC, square_recv)
    total = summed(square_recv)
    for h in range(8):
        at = slice(256 * h, 256 * h + 256)
        accum = accum_ref[at].reshape(1, 256) + total[h : h + 1] / E
        new_accum_ref[at] = accum.reshape(256)
        scale = LR / (jnp.sqrt(accum) + EPS)
        new_ref[:, at] = table_ref[:, at] - grad_ref[:, at] * scale
        if h % 2 == 1:
            done = slice(256 * h - 256, 256 * h + 256)
            store(new_ref.at[:, done], new_hbm.at[:, done])
    store(new_accum_ref, new_accum_hbm)

    wait(recv_sems.at[7], NZ, hot_all_recv)
    pieces = []
    for other in range(NZ):
        piece = hot_all_recv[other]
        pieces += [piece, pltpu.roll(piece, 64, 1)]
    hot_grad = jnp.concatenate(pieces + [jnp.zeros((64, 128), F32)], axis=0).T[0:64]
    wait(recv_sems.at[5], NZ * NX, hot_total_recv)
    split = 8 * NX
    hot_total = jnp.concatenate(
        [
            jnp.sum(hot_total_recv[0:split], axis=0),
            jnp.sum(hot_total_recv[split : NZ * NX], axis=0)[:, 0:64],
        ],
        axis=1,
    )
    accum = hot_accum_ref[...].reshape(1, 192) + hot_total / E
    new_hot_accum_ref[...] = accum.reshape(192)
    store(new_hot_accum_ref, new_hot_accum_hbm)
    new_hot_ref[...] = hot_table_ref[...] - hot_grad[:, 0:192] * (LR / (jnp.sqrt(accum) + EPS))
    store(new_hot_ref, new_hot_hbm)

    for stage, count, send in (
        (0, NC, bags_send),
        (1, NY, rows_y_send),
        (2, NY * NZ, cold_send),
        (3, NZ, hot_z_send),
        (4, NZ, rows_z_send),
        (5, NZ * NX, hot_total_recv),
        (6, NY, hot_y_recv),
        (7, NZ, hot_all_recv),
        (8, NC, square_recv),
        (9, 2, hot_square_recv),
    ):
        wait(send_sems.at[stage], count, send)
    for copy in stores:
        copy.wait()


def exchange(*operands):
    hbm = pl.BlockSpec(memory_space=pltpu.HBM)
    return pl.pallas_call(
        exchange_kernel,
        out_shape=tuple(jax.ShapeDtypeStruct(a.shape, F32) for a in operands[6:]),
        in_specs=[hbm] * 10,
        out_specs=(hbm,) * 4,
        scratch_shapes=[
            *(pltpu.VMEM(a.shape, a.dtype) for a in operands),
            *(pltpu.VMEM(a.shape, F32) for a in operands[6:]),
            pltpu.VMEM((64, 2048), F32),
            pltpu.VMEM((2 * LK, 256), BF16),
            pltpu.VMEM((NC, 16, 128), BF16),
            pltpu.VMEM((NC, 16, 128), BF16),
            pltpu.VMEM((NY, 2 * NZ, 128), F32),
            pltpu.VMEM((NY, 2 * NZ, 128), F32),
            pltpu.VMEM((NZ, 8, 128), F32),
            pltpu.VMEM((NZ, 8, 128), F32),
            pltpu.VMEM((NY * NZ, 4, 128), BF16),
            pltpu.VMEM((NY * NZ, 4, 128), BF16),
            pltpu.VMEM((NZ, 8, 128), F32),
            pltpu.VMEM((NZ, 8, 128), F32),
            pltpu.VMEM((NY, 8, 128), F32),
            pltpu.VMEM((NZ, 8, 128), F32),
            pltpu.VMEM((NC, 8, 256), F32),
            pltpu.VMEM((2, 8, 128), F32),
            pltpu.VMEM((NZ * NX, 1, 128), F32),
            pltpu.SemaphoreType.DMA((10,)),
            pltpu.SemaphoreType.DMA((7,)),
            pltpu.SemaphoreType.DMA((10,)),
            pltpu.SemaphoreType.DMA((10,)),
            pltpu.SemaphoreType.REGULAR((2,)),
        ],
        compiler_params=pltpu.CompilerParams(
            collective_id=0, has_side_effects=True, vmem_limit_bytes=60 * 1024 * 1024
        ),
        name="exchange",
    )(*operands)


def write_kernel(*refs):
    sources, targets, holds, sems = refs[0:4], refs[4:8], refs[8:12], refs[12]
    rows = sources[0].shape[0] // 4
    parts = [(0, pl.ds(rows * part, rows)) for part in range(4)]
    parts += [(i, slice(None)) for i in range(1, 4)]
    loads, stores = [], []
    for n, (i, at) in enumerate(parts):
        loads.append(pltpu.make_async_copy(sources[i].at[at], holds[i].at[at], sems.at[0, n]))
        stores.append(pltpu.make_async_copy(holds[i].at[at], targets[i].at[at], sems.at[1, n]))
    for load in loads:
        load.start()
    for load, store in zip(loads, stores):
        load.wait()
        store.start()
    for store in stores:
        store.wait()


def write(*arrays):
    hbm = pl.BlockSpec(memory_space=pltpu.HBM)
    return pl.pallas_call(
        write_kernel,
        out_shape=tuple(jax.ShapeDtypeStruct(a.shape, a.dtype) for a in arrays),
        in_specs=[hbm] * 4,
        out_specs=(hbm,) * 4,
        scratch_shapes=[
            *(pltpu.VMEM(a.shape, a.dtype) for a in arrays),
            pltpu.SemaphoreType.DMA((2, 7)),
        ],
        compiler_params=pltpu.CompilerParams(vmem_limit_bytes=60 * 1024 * 1024),
        name="write",
    )(*arrays)


def on_device(
    pooled_grad,
    cold_table,
    cold_accum,
    hot_table,
    hot_accum,
    cold_owner,
    cold_row,
    cold_bag,
    hot_id,
    hot_bag,
):
    updated = exchange(
        pooled_grad.reshape(32, E),
        cold_owner.T,
        cold_row,
        cold_bag,
        hot_id,
        hot_bag,
        cold_table,
        cold_accum,
        hot_table,
        hot_accum,
    )
    return tuple(write(*updated))


def solution(mesh):
    in_specs = (
        P(("row", "col"), None, None),
        P("col", "row"),
        P("row"),
        P("col", None),
        P(),
        P("row", None),
        P("row"),
        P("row"),
        P("row"),
        P("row"),
    )
    out_specs = (P("col", "row"), P("row"), P("col", None), P())
    return jax.shard_map(
        on_device, mesh=mesh, in_specs=in_specs, out_specs=out_specs, check_vma=False
    )
```

```python
import jax
import jax.numpy as jnp
from jax import lax
from jax.experimental import pallas as pl
from jax.experimental.pallas import tpu as pltpu
from jax.sharding import PartitionSpec as P

E = 512
LR = 0.3
EPS = 1e-08
MESH = pl.DeviceIdType.MESH

NC = 8
NY = 8
NX = 4
NZ = 12
LK = 384
LH = 512
CAP = 8
F32 = jnp.float32
BF16 = jnp.bfloat16


def iota(shape, dim):
    return lax.broadcasted_iota(jnp.int32, shape, dim)


def one_hot(mask):
    return jnp.where(mask, 1.0, 0.0).astype(BF16)


def dot(a, b):
    return jnp.dot(a, b, preferred_element_type=F32)


def dot_t(a, b):
    return lax.dot_general(a, b, (((1,), (1,)), ((), ())), preferred_element_type=F32)


def exchange_kernel(
    pool_hbm,
    owner_hbm,
    row_hbm,
    bag_hbm,
    hot_id_hbm,
    hot_bag_hbm,
    table_hbm,
    accum_hbm,
    hot_table_hbm,
    hot_accum_hbm,
    new_hbm,
    new_accum_hbm,
    new_hot_hbm,
    new_hot_accum_hbm,
    pool_ref,
    owner_ref,
    row_ref,
    bag_ref,
    hot_id_ref,
    hot_bag_ref,
    table_ref,
    accum_ref,
    hot_table_ref,
    hot_accum_ref,
    new_ref,
    new_accum_ref,
    new_hot_ref,
    new_hot_accum_ref,
    grad_ref,
    land_ref,
    bags_send,
    bags_recv,
    rows_y_send,
    rows_y_recv,
    rows_z_send,
    rows_z_recv,
    cold_send,
    cold_recv,
    hot_z_send,
    hot_z_recv,
    hot_y_recv,
    hot_all_recv,
    square_recv,
    hot_square_recv,
    hot_total_recv,
    fetch_sems,
    store_sems,
    send_sems,
    recv_sems,
    relay_sems,
):
    row = lax.axis_index("row")
    col = lax.axis_index("col")
    z = lax.div(row, NY)
    y = lax.rem(row, NY)

    def along_col(k):
        other = lax.rem(col + k, NC)
        return other, {"row": row, "col": other}

    def along_y(k):
        other = lax.rem(y + k, NY)
        return other, {"row": z * NY + other, "col": col}

    def along_z(k):
        other = lax.rem(z + k, NZ)
        return other, {"row": other * NY + y, "col": col}

    def along_core(k):
        other = col + k - 2 * lax.rem(col, 2)
        return other, {"row": row, "col": other}

    def start(stage, count, along, me, send, recv):
        for k in sorted(range(1, count), key=lambda k: -min(k, count - k)):
            other, device = along(k)
            pltpu.make_async_remote_copy(
                src_ref=send.at[me if send is recv else other],
                dst_ref=recv.at[me],
                send_sem=send_sems.at[stage],
                recv_sem=recv_sems.at[stage],
                device_id=device,
                device_id_type=MESH,
            ).start()

    def wait(sem, count, ref):
        part = ref.at[pl.ds(0, count - 1)]
        pltpu.make_async_copy(part, part, sem).wait()

    fetches = [
        pltpu.make_async_copy(source, target, fetch_sems.at[i])
        for i, (source, target) in enumerate(
            (
                (pool_hbm, pool_ref),
                (owner_hbm, owner_ref),
                (row_hbm, row_ref),
                (bag_hbm, bag_ref),
                (hot_id_hbm, hot_id_ref),
                (hot_bag_hbm, hot_bag_ref),
                (table_hbm, table_ref),
                (accum_hbm, accum_ref),
                (hot_table_hbm, hot_table_ref),
                (hot_accum_hbm, hot_accum_ref),
            )
        )
    ]
    fetches[0].start()
    barrier = pltpu.get_barrier_semaphore()
    near_z, near_y = NZ // 4, NY // 4
    greeted = []
    for along, count, near in ((along_z, NZ, near_z), (along_y, NY, near_y), (along_col, NC, NC // 2)):
        steps = {k for step in range(1, near + 1) for k in (step, count - step)}
        for k in sorted(steps, key=lambda k: -min(k, count - k)):
            greeted.append(along(k)[1])
    for device in greeted:
        pl.semaphore_signal(barrier, inc=1, device_id=device, device_id_type=MESH)
    for fetch in fetches[1:]:
        fetch.start()

    def around(step_z, step_y):
        other = lax.rem(z + step_z, NZ) * NY + lax.rem(y + step_y, NY)
        return other, {"row": other, "col": col}

    def rings(first, last, act):
        def ring(i, carry):
            step_z = NZ // 2 + (1 - 2 * lax.rem(i, 2)) * lax.div(i + 1, 2)
            for step_y in (4, 3, 5, 2, 6, 1, 7, 0):
                act(*around(step_z, step_y))
            return carry

        lax.fori_loop(first, last, ring, 0)

    fetches[0].wait()

    low_lanes = iota((16, 128), 1) < 64
    for pair in range(NC // 2):
        first = pool_ref[0:16, pair * 128 : pair * 128 + 128].astype(F32)
        second = pool_ref[16:32, pair * 128 : pair * 128 + 128].astype(F32)
        bags_send[2 * pair] = jnp.where(low_lanes, first, pltpu.roll(second, 64, 1)).astype(BF16)
        bags_send[2 * pair + 1] = jnp.where(low_lanes, pltpu.roll(first, 64, 1), second).astype(BF16)
    bags_recv[col] = bags_send[col]
    pl.semaphore_wait(barrier, len(greeted))
    start(0, NC, along_col, col, bags_send, bags_recv)
    for i, (along, count, step) in enumerate(((along_z, NZ, near_z), (along_y, NY, near_y))):
        for k in (step, count - step):
            pl.semaphore_signal(
                relay_sems.at[i], inc=1, device_id=along(k)[1], device_id_type=MESH
            )

    def place_of_bag(bag):
        return ((bag >> 4) & 1) * 128 + (bag >> 5) * 16 + (bag & 15)

    for fetch in fetches[1:6]:
        fetch.wait()
    hot_id = hot_id_ref[...].reshape(1, LH)
    hot_line = (hot_id >> 4) * 8 + (hot_id & 7) + ((hot_id >> 3) & 1) * (NZ * 8)
    hot_rows = one_hot(iota((NZ * 16, LH), 0) == hot_line)
    hot_place = place_of_bag(hot_bag_ref[...].reshape(1, LH))
    counts = dot_t(hot_rows, one_hot(iota((256, LH), 0) == hot_place))
    counts = jnp.concatenate([counts[: NZ * 8], counts[NZ * 8 :]], axis=1)
    count_high = counts.astype(BF16)
    count_low = (counts - count_high.astype(F32)).astype(BF16)
    count_parts = jnp.concatenate([count_high, count_low], axis=0)

    owner = owner_ref[...].reshape(1, LK)
    target = iota((NY * NZ, LK), 0) == owner
    taken = one_hot(target)
    earlier = one_hot(iota((128, 128), 0) < iota((128, 128), 1))
    carry = jnp.zeros((NY * NZ, 1), F32)
    ranks = []
    for part in range(LK // 128):
        at = slice(128 * part, 128 * part + 128)
        before = dot(taken[:, at], earlier) + carry
        ranks.append(jnp.sum(jnp.where(target[:, at], before, 0.0), axis=0, keepdims=True))
        carry += jnp.sum(jnp.where(target[:, at], 1.0, 0.0), axis=1, keepdims=True)
    rank = jnp.concatenate(ranks, axis=1).astype(jnp.int32)
    owner_z, owner_y = owner >> 3, owner & 7
    half, quarter = rank >> 2, rank & 3
    table_row = row_ref[...].reshape(1, LK)
    line = owner_y * (2 * NZ) + owner_z * 2 + half
    lane = lax.rem(z, 4) * 32 + y * 4 + quarter
    in_lane = iota((128, LK), 0) == lane
    high = jnp.where(in_lane, (table_row >> 8) + 1, 0).astype(F32).astype(BF16)
    low = jnp.where(in_lane, table_row & 255, 0).astype(F32).astype(BF16)
    in_line = one_hot(iota((NY * NZ * 2, LK), 0) == line)
    codes = dot_t(in_line, high) * 256.0 + dot_t(in_line, low)
    rows_y_send[...] = codes.reshape(NY, 2 * NZ, 128)
    rows_y_recv[y] = rows_y_send[y]
    pl.semaphore_wait(relay_sems.at[0], 2)
    pl.semaphore_wait(relay_sems.at[1], 2)
    start(1, NY, along_y, y, rows_y_send, rows_y_recv)

    spot = one_hot(iota((NY * CAP, LK), 0) == half * (NY * 4) + owner_y * 4 + quarter)
    cold_place = place_of_bag(bag_ref[...].reshape(1, LK)) + 1
    weight = jnp.where(iota((16, LK), 0) == owner_z, cold_place, 0).astype(F32).astype(BF16)
    slot_place = dot_t(spot, weight).astype(jnp.int32)
    bag_number = iota((NY * CAP, 256), 1) + 1
    picks = []
    for other in range(NZ):
        pick = jnp.where(slot_place[:, other : other + 1] == bag_number, 1.0, 0.0)
        picks.append(jnp.concatenate([pick[: NY * 4], pick[NY * 4 :]], axis=1))
    pick = jnp.concatenate(picks, axis=0).astype(BF16)
    wait(recv_sems.at[0], NC, bags_recv)
    bags = bags_recv[...].reshape(128, 128).astype(F32)
    rolled = pltpu.roll(bags, 64, 1)
    left = iota((128, 128), 1) < 64
    spread = jnp.concatenate(
        [
            jnp.where(left, bags, 0.0),
            jnp.where(left, rolled, 0.0),
            jnp.where(left, 0.0, rolled),
            jnp.where(left, 0.0, bags),
        ],
        axis=0,
    ).astype(BF16)
    hot_parts = dot(count_parts, spread)
    hot_z_send[...] = (hot_parts[: NZ * 8] + hot_parts[NZ * 8 :]).reshape(NZ, 8, 128)
    start(3, NZ, along_z, z, hot_z_send, hot_z_recv)
    hot_z_recv[z] = hot_z_send[z]

    wait(recv_sems.at[1], NY, rows_y_recv)
    merged = jnp.sum(rows_y_recv[...], axis=0)
    for other in range(NZ):
        rows_z_send[other, 0:2] = merged[2 * other : 2 * other + 2]
        rows_z_send[other, 2:8] = jnp.zeros((6, 128), F32)
    rows_z_recv[z] = rows_z_send[z]
    start(4, NZ, along_z, z, rows_z_send, rows_z_recv)

    cold_send[...] = dot(pick, spread).reshape(NY * NZ, 4, 128).astype(BF16)
    cold_recv[row] = cold_send[row]

    def send_cold(other, device):
        pltpu.make_async_remote_copy(
            src_ref=cold_send.at[other],
            dst_ref=cold_recv.at[row],
            send_sem=send_sems.at[2],
            recv_sem=recv_sems.at[2],
            device_id=device,
            device_id_type=MESH,
        ).start()

    rings(0, 7, send_cold)

    wait(recv_sems.at[3], NZ, hot_z_recv)
    hot_y_recv[y] = jnp.sum(hot_z_recv[...], axis=0)
    start(6, NY, along_y, y, hot_y_recv, hot_y_recv)

    rings(7, NZ - 1, send_cold)
    for step_y in (4, 3, 5, 2, 6, 1, 7):
        send_cold(*around(0, step_y))

    wait(recv_sems.at[4], NZ, rows_z_recv)
    code = jnp.concatenate(
        [jnp.sum(rows_z_recv[4 * g : 4 * g + 4], axis=0) for g in range(NZ // 4)], axis=1
    ).astype(jnp.int32)
    code_high, code_low = code >> 8, code & 255
    low_number = iota((256, LK), 0)
    land = jnp.concatenate(
        [jnp.where(code_low[side : side + 1] == low_number, 1.0, 0.0).T for side in range(2)], axis=0
    )
    land_ref[...] = land.astype(BF16)

    wait(recv_sems.at[6], NY, hot_y_recv)
    hot_mine = jnp.sum(hot_y_recv[...], axis=0)
    core, chip_x = lax.rem(col, 2), lax.div(col, 2)
    hot_square_recv[core] = hot_mine * hot_mine
    start(9, 2, along_core, core, hot_square_recv, hot_square_recv)
    hot_all_recv[z] = hot_mine
    start(7, NZ, along_z, z, hot_all_recv, hot_all_recv)

    wait(recv_sems.at[9], 2, hot_square_recv)
    total = hot_square_recv[0] + hot_square_recv[1]
    sub, at_lane = iota((8, 128), 0), iota((8, 128), 1)
    first = jnp.sum(jnp.where(at_lane < 64, total, 0.0), axis=1, keepdims=True)
    second = jnp.sum(jnp.where(at_lane < 64, 0.0, total), axis=1, keepdims=True)
    both = jnp.where(((at_lane >> 3) & 1) == 0, first, second)
    here = ((at_lane & 7) == sub) & ((at_lane >> 4) == lax.rem(z, 8))
    mine_at = z * NX + chip_x
    hot_total_recv[mine_at] = jnp.sum(jnp.where(here, both, 0.0), axis=0, keepdims=True)

    def send_total(step_z, step_x):
        device = {
            "row": lax.rem(z + step_z, NZ) * NY + y,
            "col": lax.rem(chip_x + step_x, NX) * 2 + core,
        }
        pltpu.make_async_remote_copy(
            src_ref=hot_total_recv.at[mine_at],
            dst_ref=hot_total_recv.at[mine_at],
            send_sem=send_sems.at[5],
            recv_sem=recv_sems.at[5],
            device_id=device,
            device_id_type=MESH,
        ).start()

    by_distance = sorted(
        ((step_z, step_x) for step_z in range(NZ) for step_x in range(NX)),
        key=lambda s: -(min(s[0], NZ - s[0]) + min(s[1], NX - s[1])),
    )[:-1]
    for steps in by_distance[:18]:
        send_total(*steps)

    wait(recv_sems.at[2], NY * NZ, cold_recv)
    arrived = cold_recv[...].astype(F32).reshape(LK, 128).T
    masked = []
    for side in range(2):
        mine = arrived[64 * side : 64 * side + 64]
        blocks = [jnp.where(code_high[side : side + 1] == h + 1, mine, 0.0) for h in range(8)]
        masked.append(jnp.concatenate(blocks, axis=0).astype(BF16))
    grads = dot(jnp.concatenate(masked, axis=1), land_ref[...])
    squares = []
    for h in range(8):
        part = grads[64 * h : 64 * h + 64]
        grad_ref[:, 256 * h : 256 * h + 256] = part
        squares.append(jnp.sum(part * part, axis=0, keepdims=True))
    square_recv[col] = jnp.concatenate(squares, axis=0)
    start(8, NC, along_col, col, square_recv, square_recv)

    def summed(ref):
        total = ref[0]
        for other in range(1, NC):
            total += ref[other]
        return total

    for steps in by_distance[18:]:
        send_total(*steps)
    for fetch in fetches[6:]:
        fetch.wait()

    stores = []

    def store(source, target):
        copy = pltpu.make_async_copy(source, target, store_sems.at[len(stores)])
        copy.start()
        stores.append(copy)

    wait(recv_sems.at[8], NC, square_recv)
    total = summed(square_recv)
    for h in range(8):
        at = slice(256 * h, 256 * h + 256)
        accum = accum_ref[at].reshape(1, 256) + total[h : h + 1] / E
        new_accum_ref[at] = accum.reshape(256)
        scale = LR / (jnp.sqrt(accum) + EPS)
        new_ref[:, at] = table_ref[:, at] - grad_ref[:, at] * scale
        if h % 2 == 1:
            done = slice(256 * h - 256, 256 * h + 256)
            store(new_ref.at[:, done], new_hbm.at[:, done])
    store(new_accum_ref, new_accum_hbm)

    wait(recv_sems.at[7], NZ, hot_all_recv)
    pieces = []
    for other in range(NZ):
        piece = hot_all_recv[other]
        pieces += [piece, pltpu.roll(piece, 64, 1)]
    hot_grad = jnp.concatenate(pieces + [jnp.zeros((64, 128), F32)], axis=0).T[0:64]
    wait(recv_sems.at[5], NZ * NX, hot_total_recv)
    split = 8 * NX
    hot_total = jnp.concatenate(
        [
            jnp.sum(hot_total_recv[0:split], axis=0),
            jnp.sum(hot_total_recv[split : NZ * NX], axis=0)[:, 0:64],
        ],
        axis=1,
    )
    accum = hot_accum_ref[...].reshape(1, 192) + hot_total / E
    new_hot_accum_ref[...] = accum.reshape(192)
    store(new_hot_accum_ref, new_hot_accum_hbm)
    new_hot_ref[...] = hot_table_ref[...] - hot_grad[:, 0:192] * (LR / (jnp.sqrt(accum) + EPS))
    store(new_hot_ref, new_hot_hbm)

    for stage, count, send in (
        (0, NC, bags_send),
        (1, NY, rows_y_send),
        (2, NY * NZ, cold_send),
        (3, NZ, hot_z_send),
        (4, NZ, rows_z_send),
        (5, NZ * NX, hot_total_recv),
        (6, NY, hot_y_recv),
        (7, NZ, hot_all_recv),
        (8, NC, square_recv),
        (9, 2, hot_square_recv),
    ):
        wait(send_sems.at[stage], count, send)
    for copy in stores:
        copy.wait()


def exchange(*operands):
    hbm = pl.BlockSpec(memory_space=pltpu.HBM)
    return pl.pallas_call(
        exchange_kernel,
        out_shape=tuple(jax.ShapeDtypeStruct(a.shape, F32) for a in operands[6:]),
        in_specs=[hbm] * 10,
        out_specs=(hbm,) * 4,
        scratch_shapes=[
            *(pltpu.VMEM(a.shape, a.dtype) for a in operands),
            *(pltpu.VMEM(a.shape, F32) for a in operands[6:]),
            pltpu.VMEM((64, 2048), F32),
            pltpu.VMEM((2 * LK, 256), BF16),
            pltpu.VMEM((NC, 16, 128), BF16),
            pltpu.VMEM((NC, 16, 128), BF16),
            pltpu.VMEM((NY, 2 * NZ, 128), F32),
            pltpu.VMEM((NY, 2 * NZ, 128), F32),
            pltpu.VMEM((NZ, 8, 128), F32),
            pltpu.VMEM((NZ, 8, 128), F32),
            pltpu.VMEM((NY * NZ, 4, 128), BF16),
            pltpu.VMEM((NY * NZ, 4, 128), BF16),
            pltpu.VMEM((NZ, 8, 128), F32),
            pltpu.VMEM((NZ, 8, 128), F32),
            pltpu.VMEM((NY, 8, 128), F32),
            pltpu.VMEM((NZ, 8, 128), F32),
            pltpu.VMEM((NC, 8, 256), F32),
            pltpu.VMEM((2, 8, 128), F32),
            pltpu.VMEM((NZ * NX, 1, 128), F32),
            pltpu.SemaphoreType.DMA((10,)),
            pltpu.SemaphoreType.DMA((7,)),
            pltpu.SemaphoreType.DMA((10,)),
            pltpu.SemaphoreType.DMA((10,)),
            pltpu.SemaphoreType.REGULAR((2,)),
        ],
        compiler_params=pltpu.CompilerParams(
            collective_id=0, has_side_effects=True, vmem_limit_bytes=60 * 1024 * 1024
        ),
        name="exchange",
    )(*operands)


def write_kernel(*refs):
    sources, targets, holds, sems = refs[0:4], refs[4:8], refs[8:12], refs[12]
    rows = sources[0].shape[0] // 4
    parts = [(0, pl.ds(rows * part, rows)) for part in range(4)]
    parts += [(i, slice(None)) for i in range(1, 4)]
    loads, stores = [], []
    for n, (i, at) in enumerate(parts):
        loads.append(pltpu.make_async_copy(sources[i].at[at], holds[i].at[at], sems.at[0, n]))
        stores.append(pltpu.make_async_copy(holds[i].at[at], targets[i].at[at], sems.at[1, n]))
    for load in loads:
        load.start()
    for load, store in zip(loads, stores):
        load.wait()
        store.start()
    for store in stores:
        store.wait()


def write(*arrays):
    hbm = pl.BlockSpec(memory_space=pltpu.HBM)
    return pl.pallas_call(
        write_kernel,
        out_shape=tuple(jax.ShapeDtypeStruct(a.shape, a.dtype) for a in arrays),
        in_specs=[hbm] * 4,
        out_specs=(hbm,) * 4,
        scratch_shapes=[
            *(pltpu.VMEM(a.shape, a.dtype) for a in arrays),
            pltpu.SemaphoreType.DMA((2, 7)),
        ],
        compiler_params=pltpu.CompilerParams(vmem_limit_bytes=60 * 1024 * 1024),
        name="write",
    )(*arrays)


def on_device(
    pooled_grad,
    cold_table,
    cold_accum,
    hot_table,
    hot_accum,
    cold_owner,
    cold_row,
    cold_bag,
    hot_id,
    hot_bag,
):
    updated = exchange(
        pooled_grad.reshape(32, E),
        cold_owner.T,
        cold_row,
        cold_bag,
        hot_id,
        hot_bag,
        cold_table,
        cold_accum,
        hot_table,
        hot_accum,
    )
    return tuple(write(*updated))


def solution(mesh):
    in_specs = (
        P(("row", "col"), None, None),
        P("col", "row"),
        P("row"),
        P("col", None),
        P(),
        P("row", None),
        P("row"),
        P("row"),
        P("row"),
        P("row"),
    )
    out_specs = (P("col", "row"), P("row"), P("col", None), P())
    return jax.shard_map(
        on_device, mesh=mesh, in_specs=in_specs, out_specs=out_specs, check_vma=False
    )
```
